32 devices in a mesh: vert: 4 (over z), feat: 8 (over y, x, core).
Axes of the slice: x: 2, y: 2, z: 4, core: 2. Of those that a mesh axis runs over, the one named last changes fastest.
Arguments:
- states: bfloat16 [4, 256, 16384], P(None, 'feat', 'vert'), may hold values from -6 to 6
- depth_weight: float32 [4, 256], P(None, 'feat'), may hold values from -1 to 1
- tile_values: bfloat16 [4, 256, 128, 128], P('vert'), may hold values from -0.1875 to 0.1875
- tile_dst: int32 [4, 256], P('vert'), may hold values from 0 to 31
- tile_src: int32 [4, 256], P('vert'), may hold values from 0 to 33
- tile_count: int32 [4], P('vert'), may hold values from 64 to 256, as said below
- send_rows: int32 [4, 4, 64], P('vert'), may hold values from 0 to 4095
- weight: bfloat16 [256, 256], replicated, may hold values from -0.375 to 0.375
- bias_vec: float32 [256], P('feat'), may hold values from -3 to 3
- cotangent: bfloat16 [256, 16384], P('feat', 'vert'), may hold values from -6 to 6
Outputs:
- layer_out: bfloat16 [256, 16384], P('feat', 'vert')
- grad_states: bfloat16 [4, 256, 16384], P(None, 'feat', 'vert')
- grad_weight: float32 [256, 256], P('feat')
- grad_bias: float32 [256], P('feat')
- grad_depth: float32 [4, 256], P(None, 'feat')
The draws below stay inside these ranges and needn't reach their ends.
Inputs may be any that keep to these rules, and one draw needn't show every extreme that they name: `tile_count`: at least 64 tiles in every partition, and exactly 256 in some partition.
All inputs are finite; a program needn't handle non-finite values.
Results may differ from the reference program's by a relative error of at most 0.024.
Values may be sent and summed in bfloat16 or wider, within the bound.
A program may use at most 64 MiB of HBM per device.

```python
import math
import jax
import jax.numpy as jnp
from jax import lax

D = 256
STATES = 4
BLOCK = 128
HALO = 64
ROWS = 4096
SECTIONS = 4
TILE_CAP = 256
VERTICES = 16384


def draw_tile_count(key, part):
    first_key, second_key = jax.random.split(jax.random.fold_in(key, 7))
    counts = jax.random.randint(first_key, (SECTIONS,), TILE_CAP // 4, TILE_CAP + 1, dtype=jnp.int32)
    fullest = jax.random.randint(second_key, (), 0, SECTIONS, dtype=jnp.int32)
    return jnp.where(jnp.arange(SECTIONS, dtype=jnp.int32) == fullest, jnp.int32(TILE_CAP), counts).astype(jnp.int32)


def set_ends(drawn, own_key, smallest, top_value):
    longest = drawn.shape.index(max(drawn.shape))
    spots = []
    for shift in (0, 1):
        where = [jax.random.randint(jax.random.fold_in(own_key, axis), (), 0, length) for axis, length in enumerate(drawn.shape)]
        where[longest] = (where[longest] + shift) % drawn.shape[longest]
        spots.append(tuple(where))
    return drawn.at[spots[0]].set(smallest).at[spots[1]].set(top_value)


def level_of(stream_key, dims, cuts, smallest, largest):
    loudness, own = 1.0, jax.random.fold_in(stream_key, 6)
    for dim, shards_of in cuts:
        draws = jnp.exp(jax.random.uniform(jax.random.fold_in(own, dim), (shards_of,), jnp.float32, smallest / len(cuts), largest / len(cuts)))
        loudness = loudness * jnp.repeat(draws, dims[dim] // shards_of).reshape([-1 if axis == dim else 1 for axis in range(len(dims))])
    return loudness


def bell_draw(stream_key, dims, width, limit, cuts=(), held_as=jnp.bfloat16):
    gain = level_of(stream_key, dims, cuts, -0.22, 0.18) if cuts else 1.0
    entries = jax.random.normal(stream_key, dims, jnp.float32) * width * gain
    return jnp.minimum(jnp.maximum(entries, -limit), limit).astype(held_as)


def setup_inputs(seed: int = 0) -> dict:
    key_list = jax.random.split(jax.random.key(seed), 11)
    states = bell_draw(key_list[0], (STATES, D, VERTICES), 1.0, 6.0, ((1, 8), (2, 4)))
    depth_weight = jnp.clip(jax.random.uniform(key_list[1], (STATES, D), jnp.float32, -1.0, 1.0) * level_of(key_list[1], (STATES, D), ((1, 8),), -0.4, 0.0), -1.0, 1.0)
    tile_values = bell_draw(key_list[2], (SECTIONS, TILE_CAP, BLOCK, BLOCK), (8 * BLOCK) ** -0.5, 0.1875, ((0, 4),))
    tile_dst = set_ends(jax.random.randint(key_list[3], (SECTIONS, TILE_CAP), 0, ROWS // BLOCK), jax.random.fold_in(key_list[3], 1), 0, (ROWS // BLOCK) - 1).astype(jnp.int32)
    tile_src = set_ends(jax.random.randint(key_list[4], (SECTIONS, TILE_CAP), 0, (ROWS + SECTIONS * HALO) // BLOCK), jax.random.fold_in(key_list[4], 1), 0, ((ROWS + SECTIONS * HALO) // BLOCK) - 1).astype(jnp.int32)
    tile_count = draw_tile_count(jax.random.fold_in(key_list[10], 71), 0)
    send_rows = set_ends(jax.random.randint(key_list[6], (SECTIONS, SECTIONS, HALO), 0, ROWS), jax.random.fold_in(key_list[6], 1), 0, ROWS - 1).astype(jnp.int32)
    weight = bell_draw(key_list[7], (D, D), D ** -0.5, 0.375)
    bias_vec = bell_draw(key_list[8], (D,), 0.5, 3.0, ((0, 8),), jnp.float32)
    cotangent = bell_draw(key_list[9], (D, VERTICES), 1.0, 6.0, ((0, 8), (1, 4)))
    return dict(states=states, depth_weight=depth_weight, tile_values=tile_values, tile_dst=tile_dst, tile_src=tile_src, tile_count=tile_count, send_rows=send_rows, weight=weight, bias_vec=bias_vec, cotangent=cotangent)


def halo_columns(send_rows, section):
    base = jnp.arange(SECTIONS, dtype=jnp.int32)[:, None] * ROWS
    return (base + send_rows[:, section, :]).reshape(-1).astype(jnp.int32)

def aggregate(mixed_state, tile_values, tile_dst, tile_src, tile_count, send_rows):
    row_blocks = ROWS // BLOCK
    src_blocks = (ROWS + SECTIONS * HALO) // BLOCK

    def one_part(section):
        local_part = lax.dynamic_slice_in_dim(mixed_state, (section * ROWS).astype(jnp.int32), ROWS, 1)
        halo_part = jnp.take(mixed_state, halo_columns(send_rows, section), axis=1)
        extended = jnp.concatenate([local_part, halo_part], axis=1).reshape(D, src_blocks, BLOCK)
        picked = jnp.take(extended, tile_src[section], axis=1).astype(jnp.float32)
        products = jnp.einsum('dtc,trc->dtr', picked, tile_values[section].astype(jnp.float32))
        live_mask = jnp.arange(TILE_CAP, dtype=jnp.int32) < tile_count[section]
        onehot = ((tile_dst[section][:, None] == jnp.arange(row_blocks, dtype=jnp.int32)[None, :]) & live_mask[:, None]).astype(jnp.float32)
        return jnp.einsum('dtr,tn->dnr', products, onehot).reshape(D, ROWS)
    parted = lax.map(one_part, jnp.arange(SECTIONS, dtype=jnp.int32))
    return jnp.transpose(parted, (1, 0, 2)).reshape(D, SECTIONS * ROWS)

def spread(grad_agg, tile_values, tile_dst, tile_src, tile_count, send_rows):
    row_blocks = ROWS // BLOCK
    src_blocks = (ROWS + SECTIONS * HALO) // BLOCK

    def one_part(running, section):
        start_col = (section * ROWS).astype(jnp.int32)
        local_grad = lax.dynamic_slice_in_dim(grad_agg, start_col, ROWS, 1).reshape(D, row_blocks, BLOCK)
        picked = jnp.take(local_grad, tile_dst[section], axis=1).astype(jnp.float32)
        products = jnp.einsum('dtr,trc->dtc', picked, tile_values[section].astype(jnp.float32))
        live_mask = jnp.arange(TILE_CAP, dtype=jnp.int32) < tile_count[section]
        onehot = ((tile_src[section][:, None] == jnp.arange(src_blocks, dtype=jnp.int32)[None, :]) & live_mask[:, None]).astype(jnp.float32)
        extended = jnp.einsum('dtc,ts->dsc', products, onehot).reshape(D, src_blocks * BLOCK)
        halo_terms = lax.optimization_barrier(extended[:, ROWS:].astype(jnp.bfloat16)).astype(jnp.float32)
        own_now = lax.dynamic_slice_in_dim(running, start_col, ROWS, 1)
        running = lax.dynamic_update_slice_in_dim(running, own_now + extended[:, :ROWS], start_col, 1)
        running = running.at[:, halo_columns(send_rows, section)].add(halo_terms)
        return (running, None)
    start = jnp.zeros((D, SECTIONS * ROWS), jnp.float32)
    result, unused = lax.scan(one_part, start, jnp.arange(SECTIONS, dtype=jnp.int32))
    return result

def reference(states, depth_weight, tile_values, tile_dst, tile_src, tile_count, send_rows, weight, bias_vec, cotangent):
    norm_scale = 1.0 / math.sqrt(VERTICES)
    states32 = states.astype(jnp.float32)
    mixed_state = lax.optimization_barrier(jnp.sum(depth_weight[:, :, None] * states32, axis=0)).astype(jnp.bfloat16)
    aggregated = aggregate(mixed_state, tile_values, tile_dst, tile_src, tile_count, send_rows).astype(jnp.bfloat16)
    pre_act = jnp.dot(weight.T, aggregated, preferred_element_type=jnp.float32) + bias_vec[:, None]
    sigmoid_pre = jax.nn.sigmoid(pre_act)
    layer_out = (pre_act * sigmoid_pre).astype(jnp.bfloat16)
    grad_pre = (cotangent.astype(jnp.float32) * sigmoid_pre * (1.0 + pre_act * (1.0 - sigmoid_pre))).astype(jnp.bfloat16)
    grad_agg = jnp.dot(weight, grad_pre, preferred_element_type=jnp.float32).astype(jnp.bfloat16)
    grad_weight = jnp.dot(aggregated, grad_pre.T, preferred_element_type=jnp.float32) * norm_scale
    grad_bias = lax.optimization_barrier(jnp.sum(grad_pre.astype(jnp.float32), axis=1)) * norm_scale
    grad_mixed = spread(grad_agg, tile_values, tile_dst, tile_src, tile_count, send_rows)
    grad_states = (depth_weight[:, :, None] * grad_mixed[None]).astype(jnp.bfloat16)
    grad_depth = lax.optimization_barrier(jnp.sum(states32 * grad_mixed[None], axis=2)) * norm_scale
    return (layer_out, grad_states, grad_weight, grad_bias, grad_depth)
```

```python
import functools
import math

import jax
import jax.numpy as jnp
from jax import lax
from jax.experimental import pallas as pl
from jax.experimental.pallas import tpu as pltpu
from jax.sharding import PartitionSpec as P

F32 = jnp.float32
BF16 = jnp.bfloat16
HALO_OUT, COT, BIAS, AGG, GRAD, LAYER, TERMS, HALO_BACK, SUMS, DEPTH = range(10)
TILE_PARTS = 8
UNROLL = 8


def whole_kernel(
    sizes,
    norm_scale,
    order_ref,
    block_ref,
    keep_ref,
    last_ref,
    has_ref,
    states_ref,
    depth_ref,
    rows_ref,
    rows_col_ref,
    weight_ref,
    bias_ref,
    cot_ref,
    tiles_hbm,
    layer_ref,
    grad_states_ref,
    grad_weight_ref,
    grad_bias_ref,
    grad_depth_ref,
    tiles,
    extended,
    running,
    halo_send,
    halo_recv,
    back_send,
    back_recv,
    cot_recv,
    bias_recv,
    agg_send,
    agg_recv,
    grad_send,
    grad_recv,
    layer_send,
    layer_recv,
    terms_send,
    terms_recv,
    sums_recv,
    depth_recv,
    grad_blocks,
    mixed_grad,
    weight_t,
    tile_sem,
    send_sem,
    recv_sem,
):
    vert, feat, channels, row_count, block, halo = sizes
    state_count = states_ref.shape[0]
    capacity = tiles.shape[0]
    width = row_count // feat
    features = channels * feat
    row_blocks = row_count // block
    src_blocks = extended.shape[0]
    slots = vert * halo
    per_block = block // halo
    per_width = width // block
    my_vert = lax.axis_index("vert")
    my_feat = lax.axis_index("feat")

    def vert_peer(k):
        return lax.rem(my_vert + k, vert)

    def feat_peer(k):
        return lax.rem(my_feat + k, feat)

    def vert_copy(kind, k, src, dst):
        return pltpu.make_async_remote_copy(
            src_ref=src,
            dst_ref=dst,
            send_sem=send_sem.at[kind, k],
            recv_sem=recv_sem.at[kind, k],
            device_id=(vert_peer(k), my_feat),
            device_id_type=pl.DeviceIdType.MESH,
        )

    def feat_copy(kind, k, src, dst):
        return pltpu.make_async_remote_copy(
            src_ref=src,
            dst_ref=dst,
            send_sem=send_sem.at[kind, k],
            recv_sem=recv_sem.at[kind, k],
            device_id=(my_vert, feat_peer(k)),
            device_id_type=pl.DeviceIdType.MESH,
        )

    def vert_exchange(kind, send, recv):
        copies = [
            vert_copy(kind, k, send.at[vert_peer(k)], recv.at[my_vert]) for k in range(1, vert)
        ]
        for copy in copies:
            copy.start()
        return copies

    def vert_spread(kind, recv):
        copies = [
            vert_copy(kind, k, recv.at[my_vert], recv.at[my_vert]) for k in range(1, vert)
        ]
        for copy in copies:
            copy.start()
        return copies

    def feat_exchange(kind, send, recv):
        copies = [
            feat_copy(kind, k, send.at[feat_peer(k)], recv.at[my_feat]) for k in range(1, feat)
        ]
        for copy in copies:
            copy.start()
        return copies

    def arrived(copies):
        for copy in copies:
            copy.wait_recv()

    barrier = pltpu.get_barrier_semaphore()
    for k in range(1, vert):
        pl.semaphore_signal(
            barrier, inc=1, device_id=(vert_peer(k), my_feat), device_id_type=pl.DeviceIdType.MESH
        )
    for k in range(1, feat):
        pl.semaphore_signal(
            barrier, inc=1, device_id=(my_vert, feat_peer(k)), device_id_type=pl.DeviceIdType.MESH
        )

    part = capacity // TILE_PARTS
    tile_copies = [
        pltpu.make_async_copy(
            tiles_hbm.at[0, pl.ds(i * part, part)], tiles.at[pl.ds(i * part, part)], tile_sem.at[i]
        )
        for i in range(TILE_PARTS)
    ]
    for copy in tile_copies:
        copy.start()

    depth = [depth_ref[:, j : j + 1] for j in range(state_count)]
    rows = rows_ref[...]
    step = 2 * block

    def mix(i, picked):
        start = pl.multiple_of(i * step, step)
        total = depth[0] * states_ref[0, :, pl.ds(start, step)].astype(F32)
        for j in range(1, state_count):
            total += depth[j] * states_ref[j, :, pl.ds(start, step)].astype(F32)
        mixed = total.astype(BF16)
        extended[2 * i] = mixed[:, :block]
        extended[2 * i + 1] = mixed[:, block:]
        here = lax.broadcasted_iota(jnp.int32, (step, slots), 0) + start
        onehot = jnp.where(here == rows, 1.0, 0.0).astype(BF16)
        return picked + jnp.dot(mixed, onehot, preferred_element_type=F32)

    picked = lax.fori_loop(
        0, row_count // step, mix, jnp.zeros((channels, slots), F32), unroll=2
    ).astype(BF16)
    for p in range(vert):
        halo_send[p] = picked[:, p * halo : (p + 1) * halo]

    pl.semaphore_wait(barrier, vert + feat - 2)
    halo_copies = vert_exchange(HALO_OUT, halo_send, halo_recv)
    cot_copies = [
        feat_copy(
            COT,
            k,
            cot_ref.at[:, pl.ds(pl.multiple_of(feat_peer(k) * width, width), width)],
            cot_recv.at[my_feat],
        )
        for k in range(1, feat)
    ]
    bias_recv[my_feat] = bias_ref[...]
    bias_copies = [
        feat_copy(BIAS, k, bias_recv.at[my_feat], bias_recv.at[my_feat]) for k in range(1, feat)
    ]
    for copy in cot_copies + bias_copies:
        copy.start()
    halo_recv[my_vert] = halo_send[my_vert]
    cot_recv[my_feat] = cot_ref[:, pl.ds(pl.multiple_of(my_feat * width, width), width)]
    weight = weight_ref[...]
    weight_t[...] = weight.astype(F32).T.astype(BF16)

    arrived(halo_copies)
    for j in range(src_blocks - row_blocks):
        extended[row_blocks + j] = jnp.concatenate(
            [halo_recv[j * per_block + h] for h in range(per_block)], axis=1
        )
    for copy in tile_copies:
        copy.wait()

    def tile_pass(base, source, dims):
        def group(g, total):
            for u in range(UNROLL):
                k = g * UNROLL + u
                product = lax.dot_general(
                    source[block_ref[base + k]],
                    tiles[order_ref[base + k]],
                    (dims, ((), ())),
                    preferred_element_type=F32,
                )
                total = total * keep_ref[base + k] + product
                running[k] = total
            return total

        lax.fori_loop(0, capacity // UNROLL, group, jnp.zeros((channels, block), F32))

    tile_pass(0, extended, ((1,), (1,)))
    for n in range(row_blocks):
        j = n % per_width
        agg_send[n // per_width, :, j * block : (j + 1) * block] = (
            running[last_ref[n]] * has_ref[n]
        ).astype(BF16)
    agg_copies = feat_exchange(AGG, agg_send, agg_recv)
    agg_recv[my_feat] = agg_send[my_feat]
    arrived(cot_copies)
    arrived(bias_copies)
    arrived(agg_copies)

    aggregated = agg_recv[...].reshape(features, width)
    bias = bias_recv[...].reshape(features, block)[:, :1]
    pre_act = jnp.dot(weight_t[...], aggregated, preferred_element_type=F32) + bias
    sigmoid_pre = jax.nn.sigmoid(pre_act)
    grad_pre32 = (
        cot_recv[...].reshape(features, width).astype(F32)
        * sigmoid_pre
        * (1.0 + pre_act * (1.0 - sigmoid_pre))
    )
    grad_pre = grad_pre32.astype(BF16)
    grad_send[...] = (
        jnp.dot(weight, grad_pre, preferred_element_type=F32)
        .astype(BF16)
        .reshape(feat, channels, width)
    )
    grad_copies = feat_exchange(GRAD, grad_send, grad_recv)
    grad_recv[my_feat] = grad_send[my_feat]
    layer_send[...] = (pre_act * sigmoid_pre).astype(BF16).reshape(feat, channels, width)
    layer_copies = feat_exchange(LAYER, layer_send, layer_recv)
    layer_recv[my_feat] = layer_send[my_feat]
    terms_send[:, :, :features] = lax.dot_general(
        aggregated, grad_pre, (((1,), (1,)), ((), ())), preferred_element_type=F32
    ).reshape(feat, channels, features)
    terms_send[:, :, features:] = jnp.broadcast_to(
        jnp.sum(grad_pre.astype(F32), axis=1, keepdims=True), (features, block)
    ).reshape(feat, channels, block)
    terms_copies = feat_exchange(TERMS, terms_send, terms_recv)
    terms_recv[my_feat] = terms_send[my_feat]

    arrived(grad_copies)
    for n in range(row_blocks):
        j = n % per_width
        grad_blocks[n] = grad_recv[n // per_width, :, j * block : (j + 1) * block]
    tile_pass(capacity, grad_blocks, ((1,), (0,)))

    for s in range(row_blocks, src_blocks):
        value = (running[last_ref[src_blocks + s]] * has_ref[src_blocks + s]).astype(BF16)
        for h in range(per_block):
            back_send[(s - row_blocks) * per_block + h] = value[:, h * halo : (h + 1) * halo]
    back_copies = vert_exchange(HALO_BACK, back_send, back_recv)
    back_recv[my_vert] = back_send[my_vert]
    for s in range(row_blocks):
        mixed_grad[:, s * block : (s + 1) * block] = (
            running[last_ref[src_blocks + s]] * has_ref[src_blocks + s]
        )

    arrived(terms_copies)
    total = terms_recv[0]
    for f in range(1, feat):
        total += terms_recv[f]
    sums_recv[my_vert] = total
    sums_copies = vert_spread(SUMS, sums_recv)
    arrived(layer_copies)
    for f in range(feat):
        layer_ref[:, f * width : (f + 1) * width] = layer_recv[f]

    arrived(back_copies)
    returned = jnp.concatenate([back_recv[q] for q in range(vert)], axis=1)
    rows_col = rows_col_ref[...]

    def finish(i, sums):
        start = pl.multiple_of(i * step, step)
        here = lax.broadcasted_iota(jnp.int32, (slots, step), 1) + start
        onehot = jnp.where(here == rows_col, 1.0, 0.0).astype(BF16)
        grad_mixed = mixed_grad[:, pl.ds(start, step)] + jnp.dot(
            returned, onehot, preferred_element_type=F32
        )
        out = []
        for j in range(state_count):
            grad_states_ref[j, :, pl.ds(start, step)] = (depth[j] * grad_mixed).astype(BF16)
            term = states_ref[j, :, pl.ds(start, step)].astype(F32) * grad_mixed
            term = term[:, :block] + term[:, block:]
            out.append(sums[j] + term)
        return tuple(out)

    sums = lax.fori_loop(
        0,
        row_count // step,
        finish,
        tuple(jnp.zeros((channels, block), F32) for _ in range(state_count)),
        unroll=2,
    )
    lane = lax.broadcasted_iota(jnp.int32, (channels, block), 1)
    packed = jnp.zeros((channels, block), F32)
    for j in range(state_count):
        packed = jnp.where(lane == j, jnp.sum(sums[j], axis=1, keepdims=True), packed)
    depth_recv[my_vert] = packed
    depth_copies = vert_spread(DEPTH, depth_recv)

    arrived(sums_copies)
    total = sums_recv[0]
    for q in range(1, vert):
        total += sums_recv[q]
    grad_weight_ref[...] = total[:, :features] * norm_scale
    grad_bias_ref[...] = total[:, features:] * norm_scale
    arrived(depth_copies)
    total = depth_recv[0]
    for q in range(1, vert):
        total += depth_recv[q]
    grad_depth_ref[...] = total * norm_scale
    for copies in (
        halo_copies,
        cot_copies,
        bias_copies,
        agg_copies,
        grad_copies,
        layer_copies,
        terms_copies,
        back_copies,
        sums_copies,
        depth_copies,
    ):
        for copy in copies:
            copy.wait_send()


def sort_tiles(keys, others, key_count):
    capacity = keys.shape[1]
    spot = jnp.arange(capacity, dtype=jnp.int32)
    full = keys * capacity + spot[None, :]
    rank = jnp.sum((full[:, None, :] < full[:, :, None]).astype(jnp.int32), axis=2)
    packed = (spot[None, :] * 128 + keys) * 128 + others
    chosen = rank[:, None, :] == spot[None, :, None]
    packed = jnp.sum(jnp.where(chosen, packed[:, None, :], 0), axis=2)
    order = packed // (128 * 128)
    sorted_keys = (packed // 128) % 128
    other = packed % 128
    before = jnp.concatenate([jnp.full((2, 1), -1, jnp.int32), sorted_keys[:, :-1]], axis=1)
    keep = (sorted_keys == before).astype(F32)
    bins = jnp.arange(key_count, dtype=jnp.int32)[None, :, None]
    upto = jnp.sum((keys[:, None, :] <= bins).astype(jnp.int32), axis=2)
    has = jnp.any(keys[:, None, :] == bins, axis=2).astype(F32)
    last = jnp.maximum(upto - 1, 0)
    return [a.reshape(-1) for a in (order, other, keep, last, has)]


def local(
    states,
    depth_weight,
    tile_values,
    tile_dst,
    tile_src,
    tile_count,
    send_rows,
    weight,
    bias_vec,
    cotangent,
):
    state_count, channels, row_count = states.shape
    capacity, block = tile_values.shape[1], tile_values.shape[2]
    vert, feat = lax.axis_size("vert"), lax.axis_size("feat")
    halo = send_rows.shape[2]
    slots = send_rows.shape[1] * halo
    width = row_count // feat
    features = channels * feat
    row_blocks = row_count // block
    src_blocks = (row_count + slots) // block
    norm_scale = 1.0 / math.sqrt(vert * row_count)

    live = jnp.arange(capacity, dtype=jnp.int32)[None, :] < tile_count[0]
    both = jnp.concatenate([tile_dst, tile_src], axis=0)
    keys = jnp.where(live, both, src_blocks)
    others = jnp.concatenate([tile_src, tile_dst], axis=0)
    scalars = sort_tiles(keys, others, src_blocks)

    vmem = pl.BlockSpec(memory_space=pltpu.VMEM)
    smem = pl.BlockSpec(memory_space=pltpu.SMEM)
    most = max(vert, feat)
    terms = features + block
    layer, grad_states, grad_weight, grad_bias, grad_depth = pl.pallas_call(
        functools.partial(
            whole_kernel, (vert, feat, channels, row_count, block, halo), norm_scale
        ),
        out_shape=(
            jax.ShapeDtypeStruct((channels, row_count), BF16),
            jax.ShapeDtypeStruct((state_count, channels, row_count), BF16),
            jax.ShapeDtypeStruct((channels, features), F32),
            jax.ShapeDtypeStruct((channels, block), F32),
            jax.ShapeDtypeStruct((channels, block), F32),
        ),
        in_specs=[smem] * 5 + [vmem] * 7 + [pl.BlockSpec(memory_space=pl.ANY)],
        out_specs=(vmem,) * 5,
        scratch_shapes=[
            pltpu.VMEM((capacity, block, block), BF16),
            pltpu.VMEM((src_blocks, channels, block), BF16),
            pltpu.VMEM((capacity, channels, block), F32),
            pltpu.VMEM((vert, channels, halo), BF16),
            pltpu.VMEM((vert, channels, halo), BF16),
            pltpu.VMEM((vert, channels, halo), BF16),
            pltpu.VMEM((vert, channels, halo), BF16),
            pltpu.VMEM((feat, channels, width), BF16),
            pltpu.VMEM((feat, channels, block), F32),
            pltpu.VMEM((feat, channels, width), BF16),
            pltpu.VMEM((feat, channels, width), BF16),
            pltpu.VMEM((feat, channels, width), BF16),
            pltpu.VMEM((feat, channels, width), BF16),
            pltpu.VMEM((feat, channels, width), BF16),
            pltpu.VMEM((feat, channels, width), BF16),
            pltpu.VMEM((feat, channels, terms), F32),
            pltpu.VMEM((feat, channels, terms), F32),
            pltpu.VMEM((vert, channels, terms), F32),
            pltpu.VMEM((vert, channels, block), F32),
            pltpu.VMEM((row_blocks, channels, block), BF16),
            pltpu.VMEM((channels, row_count), F32),
            pltpu.VMEM((features, features), BF16),
            pltpu.SemaphoreType.DMA((TILE_PARTS,)),
            pltpu.SemaphoreType.DMA((10, most)),
            pltpu.SemaphoreType.DMA((10, most)),
        ],
        compiler_params=pltpu.CompilerParams(
            collective_id=0, has_side_effects=True, vmem_limit_bytes=48 * 1024 * 1024
        ),
    )(
        *scalars,
        states,
        depth_weight.T,
        send_rows.reshape(1, slots),
        send_rows.reshape(slots, 1),
        weight,
        jnp.broadcast_to(bias_vec[:, None], (channels, block)),
        cotangent,
        tile_values,
    )
    return layer, grad_states, grad_weight, grad_bias[:, 0], grad_depth[:, :state_count].T


def solution(mesh):
    placed = (
        P(None, "feat", "vert"),
        P(None, "feat"),
        P("vert", None, None, None),
        P("vert", None),
        P("vert", None),
        P("vert"),
        P("vert", None, None),
        P(),
        P("feat"),
        P("feat", "vert"),
    )
    return jax.shard_map(
        local,
        mesh=mesh,
        in_specs=placed,
        out_specs=(
            P("feat", "vert"),
            P(None, "feat", "vert"),
            P("feat", None),
            P("feat"),
            P(None, "feat"),
        ),
        check_vma=False,
    )
```

```python
import functools
import math

import jax
import jax.numpy as jnp
from jax import lax
from jax.experimental import pallas as pl
from jax.experimental.pallas import tpu as pltpu
from jax.sharding import PartitionSpec as P

F32 = jnp.float32
BF16 = jnp.bfloat16
HALO_OUT, COT, BIAS, AGG, GRAD, LAYER, TERMS, HALO_BACK, SUMS, DEPTH = range(10)
TILE_PARTS = 8
GROUPS = 6
VMEM_LIMIT = 63 * 1024 * 1024
STRIDE = 128
MIX_UNROLL = 8


def diagonal(size):
    down = lax.broadcasted_iota(jnp.int32, (size, size), 0)
    return down == lax.broadcasted_iota(jnp.int32, (size, size), 1)


def column_of(row):
    size = row.shape[1]
    spread = jnp.broadcast_to(row, (size, size))
    return jnp.sum(jnp.where(diagonal(size), spread, 0.0), axis=1, keepdims=True)


def row_of(column):
    size = column.shape[0]
    spread = jnp.broadcast_to(column, (size, size))
    return jnp.sum(jnp.where(diagonal(size), spread, 0.0), axis=0, keepdims=True)


def plan_tiles(tile_total, dst, src, plan_vec):
    capacity = dst.shape[1]
    lanes = plan_vec.shape[1]
    live = lax.broadcasted_iota(jnp.int32, (1, capacity), 1) < tile_total
    dead = float(STRIDE - 1)
    dst, src = dst.astype(F32), src.astype(F32)
    dst_key, src_key = jnp.where(live, dst, dead), jnp.where(live, src, dead)
    down = lax.broadcasted_iota(jnp.int32, (STRIDE, capacity), 0)
    stacked = jnp.where(down == 0, dst_key, jnp.where(down == 1, src_key, 0.0))
    stacked = jnp.where(down == 2, dst, jnp.where(down == 3, src, stacked))
    turned = stacked.T
    square = (capacity, capacity)
    earlier = lax.broadcasted_iota(jnp.int32, square, 1) < lax.broadcasted_iota(
        jnp.int32, square, 0
    )
    place = lax.broadcasted_iota(jnp.int32, (capacity, 1), 0).astype(F32)
    bins = lax.broadcasted_iota(jnp.int32, (capacity, STRIDE), 1).astype(F32)
    spots = lax.broadcasted_iota(jnp.int32, (capacity, lanes), 1).astype(F32)
    plan_vec[...] = jnp.zeros(plan_vec.shape, jnp.int32)
    for row, key_row, key, other in (
        (0, dst_key, turned[:, 0:1], turned[:, 3:4]),
        (2, src_key, turned[:, 1:2], turned[:, 2:3]),
    ):
        same = jnp.where((key_row == key) & earlier, 1.0, 0.0)
        inside = jnp.sum(same, axis=1, keepdims=True)
        counts = jnp.sum(jnp.where(bins == key, 1.0, 0.0), axis=0, keepdims=True)
        pairs = jnp.floor((counts + 1.0) * 0.5)
        first = jnp.sum(jnp.where(bins < key, pairs, 0.0), axis=1, keepdims=True)
        spot = jnp.where(key == dead, -1.0, 2.0 * first + inside)
        word = (2.0 * place + jnp.where(inside > 0.0, 1.0, 0.0)) * STRIDE + other + 1.0
        words = jnp.sum(jnp.where(spots == spot, word, 0.0), axis=0, keepdims=True)
        plan_vec[row : row + 1, :] = words.astype(jnp.int32)
        after = jnp.floor(spot * 0.5) + 1.0
        last = jnp.max(jnp.where(bins == key, after, 0.0), axis=0, keepdims=True)
        plan_vec[row + 1 : row + 2, :STRIDE] = last.astype(jnp.int32)


def whole_kernel(
    sizes,
    norm_scale,
    count_ref,
    dst_ref,
    src_ref,
    depth_ref,
    rows_ref,
    weight_hbm,
    bias_ref,
    states_hbm,
    cot_hbm,
    tiles_hbm,
    layer_ref,
    mixed_grad,
    grad_weight_ref,
    grad_bias_ref,
    grad_depth_ref,
    tiles,
    extended,
    running,
    halo_send,
    halo_recv,
    back_send,
    back_recv,
    cot_recv,
    bias_recv,
    agg_send,
    agg_recv,
    grad_send,
    grad_recv,
    layer_send,
    layer_recv,
    terms_send,
    terms_recv,
    sums_recv,
    depth_recv,
    grad_blocks,
    weight_t,
    weight_ref,
    states_ref,
    plan_vec,
    plan,
    tile_sem,
    local_sem,
    send_sem,
    recv_sem,
):
    vert, feat, channels, row_count, block, halo = sizes
    state_count = states_ref.shape[0]
    capacity = tiles.shape[0]
    width = row_count // feat
    features = channels * feat
    row_blocks = row_count // block
    src_blocks = extended.shape[0] - 1
    unroll = (running.shape[0] - 1) // GROUPS
    slots = vert * halo
    per_block = block // halo
    per_width = width // block
    my_vert = lax.axis_index("vert")
    my_feat = lax.axis_index("feat")

    def vert_peer(k):
        return lax.rem(my_vert + k, vert)

    def feat_peer(k):
        return lax.rem(my_feat + k, feat)

    def vert_copy(kind, k, src, dst):
        return pltpu.make_async_remote_copy(
            src_ref=src,
            dst_ref=dst,
            send_sem=send_sem.at[kind, k],
            recv_sem=recv_sem.at[kind, k],
            device_id=(vert_peer(k), my_feat),
            device_id_type=pl.DeviceIdType.MESH,
        )

    def feat_copy(kind, k, src, dst):
        return pltpu.make_async_remote_copy(
            src_ref=src,
            dst_ref=dst,
            send_sem=send_sem.at[kind, k],
            recv_sem=recv_sem.at[kind, k],
            device_id=(my_vert, feat_peer(k)),
            device_id_type=pl.DeviceIdType.MESH,
        )

    def vert_exchange(kind, send, recv):
        copies = [
            vert_copy(kind, k, send.at[vert_peer(k)], recv.at[my_vert]) for k in range(1, vert)
        ]
        for copy in copies:
            copy.start()
        return copies

    def vert_spread(kind, recv):
        copies = [
            vert_copy(kind, k, recv.at[my_vert], recv.at[my_vert]) for k in range(1, vert)
        ]
        for copy in copies:
            copy.start()
        return copies

    def feat_exchange(kind, send, recv):
        copies = [
            feat_copy(kind, k, send.at[feat_peer(k)], recv.at[my_feat]) for k in range(1, feat)
        ]
        for copy in copies:
            copy.start()
        return copies

    def arrived(copies):
        for copy in copies:
            copy.wait_recv()

    barrier = pltpu.get_barrier_semaphore()
    for k in range(1, vert):
        pl.semaphore_signal(
            barrier, inc=1, device_id=(vert_peer(k), my_feat), device_id_type=pl.DeviceIdType.MESH
        )
    for k in range(1, feat):
        pl.semaphore_signal(
            barrier, inc=1, device_id=(my_vert, feat_peer(k)), device_id_type=pl.DeviceIdType.MESH
        )

    half = row_count // 2
    states_copies = [
        pltpu.make_async_copy(
            states_hbm.at[:, :, pl.ds(i * half, half)],
            states_ref.at[:, :, pl.ds(i * half, half)],
            local_sem.at[i],
        )
        for i in range(2)
    ]
    weight_copy = pltpu.make_async_copy(weight_hbm, weight_ref, local_sem.at[2])
    own_cot = pltpu.make_async_copy(
        cot_hbm.at[:, pl.ds(pl.multiple_of(my_feat * width, width), width)],
        cot_recv.at[my_feat],
        local_sem.at[3],
    )
    for copy in states_copies + [weight_copy, own_cot]:
        copy.start()
    part = capacity // TILE_PARTS
    tile_copies = [
        pltpu.make_async_copy(
            tiles_hbm.at[0, pl.ds(i * part, part)], tiles.at[pl.ds(i * part, part)], tile_sem.at[i]
        )
        for i in range(TILE_PARTS)
    ]
    for copy in tile_copies:
        copy.start()

    depth = [column_of(depth_ref[j : j + 1, :]) for j in range(state_count)]
    rows = jnp.concatenate([rows_ref[0, p : p + 1, :] for p in range(vert)], axis=1)
    extended[0] = jnp.zeros((channels, block), BF16)
    running[0] = jnp.zeros((channels, block), F32)
    step = 2 * block

    def mix(i, picked):
        start = pl.multiple_of(i * step, step)
        total = depth[0] * states_ref[0, :, pl.ds(start, step)].astype(F32)
        for j in range(1, state_count):
            total += depth[j] * states_ref[j, :, pl.ds(start, step)].astype(F32)
        mixed = total.astype(BF16)
        extended[2 * i + 1] = mixed[:, :block]
        extended[2 * i + 2] = mixed[:, block:]
        here = lax.broadcasted_iota(jnp.int32, (step, slots), 0) + start
        onehot = jnp.where(here == rows, 1.0, 0.0).astype(BF16)
        return picked + jnp.dot(mixed, onehot, preferred_element_type=F32)

    steps = row_count // step
    states_copies[0].wait()
    picked = lax.fori_loop(
        0, steps // 2, mix, jnp.zeros((channels, slots), F32), unroll=MIX_UNROLL
    )
    states_copies[1].wait()
    picked = lax.fori_loop(steps // 2, steps, mix, picked, unroll=MIX_UNROLL).astype(BF16)
    for p in range(vert):
        halo_send[p] = picked[:, p * halo : (p + 1) * halo]

    pl.semaphore_wait(barrier, vert + feat - 2)
    halo_copies = vert_exchange(HALO_OUT, halo_send, halo_recv)
    cot_copies = [
        feat_copy(
            COT,
            k,
            cot_hbm.at[:, pl.ds(pl.multiple_of(feat_peer(k) * width, width), width)],
            cot_recv.at[my_feat],
        )
        for k in range(1, feat)
    ]
    bias_recv[my_feat] = jnp.broadcast_to(column_of(bias_ref[...]), (channels, block))
    bias_copies = [
        feat_copy(BIAS, k, bias_recv.at[my_feat], bias_recv.at[my_feat]) for k in range(1, feat)
    ]
    for copy in cot_copies + bias_copies:
        copy.start()
    halo_recv[my_vert] = halo_send[my_vert]
    plan_tiles(count_ref[0], dst_ref[...], src_ref[...], plan_vec)
    plan_copy = pltpu.make_async_copy(plan_vec, plan, local_sem.at[4])
    plan_copy.start()
    weight_copy.wait()
    own_cot.wait()
    weight = weight_ref[...]
    weight_t[...] = weight.astype(F32).T.astype(BF16)

    arrived(halo_copies)
    for j in range(src_blocks - row_blocks):
        extended[row_blocks + j + 1] = jnp.concatenate(
            [halo_recv[j * per_block + h] for h in range(per_block)], axis=1
        )
    for copy in tile_copies:
        copy.wait()

    plan_copy.wait()

    def closing(row, n):
        return running[jnp.clip(plan[row, n], 0, running.shape[0] - 1)]

    def tile_pass(row, source, dims):
        def pick(k):
            word = plan[row, k]
            tile = tiles[jnp.minimum(lax.shift_right_logical(word, 8), capacity - 1)]
            own = jnp.minimum(lax.bitwise_and(word, STRIDE - 1), source.shape[0] - 1)
            return word, source[own], tile

        def group(g, total):
            for u in range(unroll):
                k = g * unroll + u
                word, left, left_tile = pick(2 * k)
                unused, right, right_tile = pick(2 * k + 1)
                product = lax.dot_general(
                    jnp.concatenate([left, right], axis=1),
                    jnp.concatenate([left_tile, right_tile], axis=dims),
                    (((1,), (dims,)), ((), ())),
                    preferred_element_type=F32,
                )
                keep = lax.bitwise_and(lax.shift_right_logical(word, 7), 1).astype(F32)
                total = total * keep + product
                running[k + 1] = total
            return total

        lax.fori_loop(0, GROUPS, group, jnp.zeros((channels, block), F32))

    tile_pass(0, extended, 1)
    for n in range(row_blocks):
        j = n % per_width
        agg_send[n // per_width, :, j * block : (j + 1) * block] = closing(1, n).astype(BF16)
    agg_copies = feat_exchange(AGG, agg_send, agg_recv)
    agg_recv[my_feat] = agg_send[my_feat]
    arrived(cot_copies)
    arrived(bias_copies)
    arrived(agg_copies)

    aggregated = agg_recv[...].reshape(features, width)
    bias = bias_recv[...].reshape(features, block)[:, :1]
    pre_act = jnp.dot(weight_t[...], aggregated, preferred_element_type=F32) + bias
    sigmoid_pre = jax.nn.sigmoid(pre_act)
    grad_pre32 = (
        cot_recv[...].reshape(features, width).astype(F32)
        * sigmoid_pre
        * (1.0 + pre_act * (1.0 - sigmoid_pre))
    )
    grad_pre = grad_pre32.astype(BF16)
    grad_send[...] = (
        jnp.dot(weight, grad_pre, preferred_element_type=F32)
        .astype(BF16)
        .reshape(feat, channels, width)
    )
    grad_copies = feat_exchange(GRAD, grad_send, grad_recv)
    grad_recv[my_feat] = grad_send[my_feat]
    layer_send[...] = (pre_act * sigmoid_pre).astype(BF16).reshape(feat, channels, width)
    layer_copies = feat_exchange(LAYER, layer_send, layer_recv)
    layer_recv[my_feat] = layer_send[my_feat]
    terms_send[:, :, :features] = lax.dot_general(
        aggregated, grad_pre, (((1,), (1,)), ((), ())), preferred_element_type=F32
    ).reshape(feat, channels, features)
    terms_send[:, :, features:] = jnp.broadcast_to(
        jnp.sum(grad_pre.astype(F32), axis=1, keepdims=True), (features, block)
    ).reshape(feat, channels, block)
    terms_copies = feat_exchange(TERMS, terms_send, terms_recv)
    terms_recv[my_feat] = terms_send[my_feat]

    grad_blocks[0] = jnp.zeros((channels, block), BF16)
    rows_col = jnp.broadcast_to(rows.astype(F32), (block, slots)).T[:, :1].astype(jnp.int32)

    arrived(grad_copies)
    for n in range(row_blocks):
        j = n % per_width
        grad_blocks[n + 1] = grad_recv[n // per_width, :, j * block : (j + 1) * block]
    tile_pass(2, grad_blocks, 0)

    for s in range(row_blocks, src_blocks):
        value = closing(3, s).astype(BF16)
        for h in range(per_block):
            back_send[(s - row_blocks) * per_block + h] = value[:, h * halo : (h + 1) * halo]
    back_copies = vert_exchange(HALO_BACK, back_send, back_recv)
    back_recv[my_vert] = back_send[my_vert]
    for s in range(row_blocks):
        mixed_grad[:, s * block : (s + 1) * block] = closing(3, s)

    arrived(terms_copies)
    total = terms_recv[0]
    for f in range(1, feat):
        total += terms_recv[f]
    sums_recv[my_vert] = total
    sums_copies = vert_spread(SUMS, sums_recv)
    arrived(layer_copies)
    for f in range(feat):
        layer_ref[:, f * width : (f + 1) * width] = layer_recv[f]

    arrived(back_copies)
    returned = jnp.concatenate([back_recv[q] for q in range(vert)], axis=1)

    def finish(i, sums):
        start = pl.multiple_of(i * step, step)
        here = lax.broadcasted_iota(jnp.int32, (slots, step), 1) + start
        onehot = jnp.where(here == rows_col, 1.0, 0.0).astype(BF16)
        grad_mixed = mixed_grad[:, pl.ds(start, step)] + jnp.dot(
            returned, onehot, preferred_element_type=F32
        )
        mixed_grad[:, pl.ds(start, step)] = grad_mixed
        out = []
        for j in range(state_count):
            term = states_ref[j, :, pl.ds(start, step)].astype(F32) * grad_mixed
            term = term[:, :block] + term[:, block:]
            out.append(sums[j] + term)
        return tuple(out)

    sums = lax.fori_loop(
        0,
        row_count // step,
        finish,
        tuple(jnp.zeros((channels, block), F32) for _ in range(state_count)),
        unroll=MIX_UNROLL,
    )
    lane = lax.broadcasted_iota(jnp.int32, (channels, block), 1)
    packed = jnp.zeros((channels, block), F32)
    for j in range(state_count):
        packed = jnp.where(lane == j, jnp.sum(sums[j], axis=1, keepdims=True), packed)
    depth_recv[my_vert] = packed
    depth_copies = vert_spread(DEPTH, depth_recv)

    arrived(sums_copies)
    total = sums_recv[0]
    for q in range(1, vert):
        total += sums_recv[q]
    grad_weight_ref[...] = total[:, :features] * norm_scale
    grad_bias_ref[...] = row_of(total[:, features : features + 1] * norm_scale)
    arrived(depth_copies)
    total = depth_recv[0]
    for q in range(1, vert):
        total += depth_recv[q]
    for j in range(state_count):
        grad_depth_ref[j : j + 1, :] = row_of(total[:, j : j + 1] * norm_scale)
    for copies in (
        halo_copies,
        cot_copies,
        bias_copies,
        agg_copies,
        grad_copies,
        layer_copies,
        terms_copies,
        back_copies,
        sums_copies,
        depth_copies,
    ):
        for copy in copies:
            copy.wait_send()


def output_kernel(
    layer, mixed_grad, grad_weight, grad_bias, grad_depth, depth_ref, layer_out, states_out, *outs
):
    layer_out[...] = layer[...]
    for ref, out in zip((grad_weight, grad_bias, grad_depth), outs):
        out[...] = ref[...]
    for j in range(depth_ref.shape[0]):
        scale = column_of(depth_ref[j : j + 1, :])
        states_out[j] = (scale * mixed_grad[...]).astype(BF16)


def local(
    states,
    depth_weight,
    tile_values,
    tile_dst,
    tile_src,
    tile_count,
    send_rows,
    weight,
    bias_vec,
    cotangent,
):
    state_count, channels, row_count = states.shape
    capacity, block = tile_values.shape[1], tile_values.shape[2]
    vert, feat = lax.axis_size("vert"), lax.axis_size("feat")
    halo = send_rows.shape[2]
    slots = send_rows.shape[1] * halo
    width = row_count // feat
    features = channels * feat
    row_blocks = row_count // block
    src_blocks = (row_count + slots) // block
    norm_scale = 1.0 / math.sqrt(vert * row_count)

    vmem = pl.BlockSpec(memory_space=pltpu.VMEM)
    smem = pl.BlockSpec(memory_space=pltpu.SMEM)
    most = max(vert, feat)
    terms = features + block
    hbm = pl.BlockSpec(memory_space=pltpu.HBM)
    pairs = -(-((capacity + src_blocks) // 2) // GROUPS) * GROUPS
    lanes = -(-2 * pairs // block) * block
    layer, mixed_grad, grad_weight, grad_bias, grad_depth = pl.pallas_call(
        functools.partial(
            whole_kernel, (vert, feat, channels, row_count, block, halo), norm_scale
        ),
        out_shape=(
            jax.ShapeDtypeStruct((channels, row_count), BF16),
            jax.ShapeDtypeStruct((channels, row_count), F32),
            jax.ShapeDtypeStruct((channels, features), F32),
            jax.ShapeDtypeStruct((1, channels), F32),
            jax.ShapeDtypeStruct((state_count, channels), F32),
        ),
        in_specs=[smem] + [vmem] * 4 + [hbm, vmem] + [hbm] * 3,
        out_specs=(vmem,) * 5,
        scratch_shapes=[
            pltpu.VMEM((capacity, block, block), BF16),
            pltpu.VMEM((src_blocks + 1, channels, block), BF16),
            pltpu.VMEM((pairs + 1, channels, block), F32),
            pltpu.VMEM((vert, channels, halo), BF16),
            pltpu.VMEM((vert, channels, halo), BF16),
            pltpu.VMEM((vert, channels, halo), BF16),
            pltpu.VMEM((vert, channels, halo), BF16),
            pltpu.VMEM((feat, channels, width), BF16),
            pltpu.VMEM((feat, channels, block), F32),
            pltpu.VMEM((feat, channels, width), BF16),
            pltpu.VMEM((feat, channels, width), BF16),
            pltpu.VMEM((feat, channels, width), BF16),
            pltpu.VMEM((feat, channels, width), BF16),
            pltpu.VMEM((feat, channels, width), BF16),
            pltpu.VMEM((feat, channels, width), BF16),
            pltpu.VMEM((feat, channels, terms), F32),
            pltpu.VMEM((feat, channels, terms), F32),
            pltpu.VMEM((vert, channels, terms), F32),
            pltpu.VMEM((vert, channels, block), F32),
            pltpu.VMEM((row_blocks + 1, channels, block), BF16),
            pltpu.VMEM((features, features), BF16),
            pltpu.VMEM((features, features), BF16),
            pltpu.VMEM((state_count, channels, row_count), BF16),
            pltpu.VMEM((8, lanes), jnp.int32),
            pltpu.SMEM((8, lanes), jnp.int32),
            pltpu.SemaphoreType.DMA((TILE_PARTS,)),
            pltpu.SemaphoreType.DMA((5,)),
            pltpu.SemaphoreType.DMA((10, most)),
            pltpu.SemaphoreType.DMA((10, most)),
        ],
        compiler_params=pltpu.CompilerParams(
            collective_id=0, has_side_effects=True, vmem_limit_bytes=VMEM_LIMIT
        ),
    )(
        tile_count,
        tile_dst,
        tile_src,
        depth_weight,
        send_rows,
        weight,
        bias_vec[None, :],
        states,
        cotangent,
        tile_values,
    )
    layer_out, grad_states, grad_weight, grad_bias, grad_depth = pl.pallas_call(
        output_kernel,
        out_shape=(
            jax.ShapeDtypeStruct((channels, row_count), BF16),
            jax.ShapeDtypeStruct((state_count, channels, row_count), BF16),
            jax.ShapeDtypeStruct((channels, features), F32),
            jax.ShapeDtypeStruct((1, channels), F32),
            jax.ShapeDtypeStruct((state_count, channels), F32),
        ),
        in_specs=[vmem] * 6,
        out_specs=(vmem,) * 5,
        compiler_params=pltpu.CompilerParams(vmem_limit_bytes=VMEM_LIMIT),
    )(layer, mixed_grad, grad_weight, grad_bias, grad_depth, depth_weight)
    return layer_out, grad_states, grad_weight, grad_bias[0], grad_depth


def solution(mesh):
    placed = (
        P(None, "feat", "vert"),
        P(None, "feat"),
        P("vert", None, None, None),
        P("vert", None),
        P("vert", None),
        P("vert"),
        P("vert", None, None),
        P(),
        P("feat"),
        P("feat", "vert"),
    )
    return jax.shard_map(
        local,
        mesh=mesh,
        in_specs=placed,
        out_specs=(
            P("feat", "vert"),
            P(None, "feat", "vert"),
            P("feat", None),
            P("feat"),
            P(None, "feat"),
        ),
        check_vma=False,
    )
```

```python
import functools
import math

import jax
import jax.numpy as jnp
from jax import lax
from jax.experimental import pallas as pl
from jax.experimental.pallas import tpu as pltpu
from jax.sharding import PartitionSpec as P

F32 = jnp.float32
BF16 = jnp.bfloat16
HALO_OUT, COT, BIAS, AGG, GRAD, LAYER, TERMS, HALO_BACK, SUMS, DEPTH = range(10)
TILE_PARTS = 8
GROUP = 10
REPEAT = 3
VMEM_LIMIT = 63 * 1024 * 1024
STRIDE = 128
MIX_UNROLL = 8


def diagonal(size):
    down = lax.broadcasted_iota(jnp.int32, (size, size), 0)
    return down == lax.broadcasted_iota(jnp.int32, (size, size), 1)


def column_of(row):
    size = row.shape[1]
    spread = jnp.broadcast_to(row, (size, size))
    return jnp.sum(jnp.where(diagonal(size), spread, 0.0), axis=1, keepdims=True)


def row_of(column):
    size = column.shape[0]
    spread = jnp.broadcast_to(column, (size, size))
    return jnp.sum(jnp.where(diagonal(size), spread, 0.0), axis=0, keepdims=True)


def plan_tiles(tile_total, dst, src, plan_vec, keep_vec):
    capacity = dst.shape[1]
    lanes = plan_vec.shape[1]
    live = lax.broadcasted_iota(jnp.int32, (1, capacity), 1) < tile_total
    dead = float(STRIDE - 1)
    dst, src = dst.astype(F32), src.astype(F32)
    dst_key, src_key = jnp.where(live, dst, dead), jnp.where(live, src, dead)
    down = lax.broadcasted_iota(jnp.int32, (STRIDE, capacity), 0)
    stacked = jnp.where(down == 0, dst_key, jnp.where(down == 1, src_key, 0.0))
    stacked = jnp.where(down == 2, dst, jnp.where(down == 3, src, stacked))
    turned = stacked.T
    square = (capacity, capacity)
    earlier = lax.broadcasted_iota(jnp.int32, square, 1) < lax.broadcasted_iota(
        jnp.int32, square, 0
    )
    place = lax.broadcasted_iota(jnp.int32, (capacity, 1), 0).astype(F32)
    bins = lax.broadcasted_iota(jnp.int32, (capacity, STRIDE), 1).astype(F32)
    spots = lax.broadcasted_iota(jnp.int32, (capacity, lanes), 1).astype(F32)
    plan_vec[...] = jnp.zeros(plan_vec.shape, jnp.int32)
    keep_vec[...] = jnp.zeros(keep_vec.shape, F32)
    for row, key_row, key, other in (
        (0, dst_key, turned[:, 0:1], turned[:, 3:4]),
        (2, src_key, turned[:, 1:2], turned[:, 2:3]),
    ):
        same = jnp.where((key_row == key) & earlier, 1.0, 0.0)
        inside = jnp.sum(same, axis=1, keepdims=True)
        counts = jnp.sum(jnp.where(bins == key, 1.0, 0.0), axis=0, keepdims=True)
        pairs = jnp.floor((counts + 1.0) * 0.5)
        first = jnp.sum(jnp.where(bins < key, pairs, 0.0), axis=1, keepdims=True)
        spot = jnp.where(key == dead, -1.0, 2.0 * first + inside)
        word = place * STRIDE + other + 1.0
        goes_on = jnp.where(inside > 0.0, 1.0, 0.0)
        keep_vec[row : row + 1, :] = jnp.sum(
            jnp.where(spots == spot, goes_on, 0.0), axis=0, keepdims=True
        )
        words = jnp.sum(jnp.where(spots == spot, word, 0.0), axis=0, keepdims=True)
        plan_vec[row : row + 1, :] = words.astype(jnp.int32)
        after = jnp.floor(spot * 0.5) + 1.0
        last = jnp.max(jnp.where(bins == key, after, 0.0), axis=0, keepdims=True)
        plan_vec[row + 1 : row + 2, :STRIDE] = last.astype(jnp.int32)


def whole_kernel(
    sizes,
    norm_scale,
    count_ref,
    dst_ref,
    src_ref,
    depth_ref,
    rows_ref,
    weight_hbm,
    bias_ref,
    states_hbm,
    cot_hbm,
    tiles_hbm,
    layer_ref,
    mixed_grad,
    grad_weight_ref,
    grad_bias_ref,
    grad_depth_ref,
    tiles,
    extended,
    running,
    halo_send,
    halo_recv,
    back_send,
    back_recv,
    cot_recv,
    bias_recv,
    agg_send,
    agg_recv,
    grad_send,
    grad_recv,
    layer_send,
    layer_recv,
    terms_send,
    terms_recv,
    sums_recv,
    depth_recv,
    grad_blocks,
    weight_t,
    weight_ref,
    states_ref,
    plan_vec,
    plan,
    keep_vec,
    keep,
    picked_states,
    tile_sem,
    local_sem,
    send_sem,
    recv_sem,
):
    vert, feat, channels, row_count, block, halo = sizes
    state_count = states_ref.shape[0]
    capacity = tiles.shape[0]
    width = row_count // feat
    features = channels * feat
    row_blocks = row_count // block
    src_blocks = extended.shape[0] - 1
    slots = vert * halo
    per_block = block // halo
    per_width = width // block
    my_vert = lax.axis_index("vert")
    my_feat = lax.axis_index("feat")

    def vert_peer(k):
        return lax.rem(my_vert + k, vert)

    def feat_peer(k):
        return lax.rem(my_feat + k, feat)

    def vert_copy(kind, k, src, dst):
        return pltpu.make_async_remote_copy(
            src_ref=src,
            dst_ref=dst,
            send_sem=send_sem.at[kind, k],
            recv_sem=recv_sem.at[kind, k],
            device_id=(vert_peer(k), my_feat),
            device_id_type=pl.DeviceIdType.MESH,
        )

    def feat_copy(kind, k, src, dst):
        return pltpu.make_async_remote_copy(
            src_ref=src,
            dst_ref=dst,
            send_sem=send_sem.at[kind, k],
            recv_sem=recv_sem.at[kind, k],
            device_id=(my_vert, feat_peer(k)),
            device_id_type=pl.DeviceIdType.MESH,
        )

    def vert_exchange(kind, send, recv):
        copies = [
            vert_copy(kind, k, send.at[vert_peer(k)], recv.at[my_vert]) for k in range(1, vert)
        ]
        for copy in copies:
            copy.start()
        return copies

    def vert_spread(kind, recv):
        copies = [
            vert_copy(kind, k, recv.at[my_vert], recv.at[my_vert]) for k in range(1, vert)
        ]
        for copy in copies:
            copy.start()
        return copies

    def feat_exchange(kind, send, recv):
        copies = [
            feat_copy(kind, k, send.at[feat_peer(k)], recv.at[my_feat]) for k in range(1, feat)
        ]
        for copy in copies:
            copy.start()
        return copies

    def arrived(copies):
        for copy in copies:
            copy.wait_recv()

    barrier = pltpu.get_barrier_semaphore()
    for k in range(1, vert):
        pl.semaphore_signal(
            barrier, inc=1, device_id=(vert_peer(k), my_feat), device_id_type=pl.DeviceIdType.MESH
        )
    for k in range(1, feat):
        pl.semaphore_signal(
            barrier, inc=1, device_id=(my_vert, feat_peer(k)), device_id_type=pl.DeviceIdType.MESH
        )

    half = row_count // 2
    states_copies = [
        pltpu.make_async_copy(
            states_hbm.at[:, :, pl.ds(i * half, half)],
            states_ref.at[:, :, pl.ds(i * half, half)],
            local_sem.at[i],
        )
        for i in range(2)
    ]
    weight_copy = pltpu.make_async_copy(weight_hbm, weight_ref, local_sem.at[2])
    own_cot = pltpu.make_async_copy(
        cot_hbm.at[:, pl.ds(pl.multiple_of(my_feat * width, width), width)],
        cot_recv.at[my_feat],
        local_sem.at[3],
    )
    for copy in states_copies + [weight_copy, own_cot]:
        copy.start()
    part = capacity // TILE_PARTS
    tile_copies = [
        pltpu.make_async_copy(
            tiles_hbm.at[0, pl.ds(i * part, part)], tiles.at[pl.ds(i * part, part)], tile_sem.at[i]
        )
        for i in range(TILE_PARTS)
    ]
    for copy in tile_copies:
        copy.start()

    depth = [column_of(depth_ref[j : j + 1, :]) for j in range(state_count)]
    rows = jnp.concatenate([rows_ref[0, p : p + 1, :] for p in range(vert)], axis=1)
    extended[0] = jnp.zeros((channels, block), BF16)
    running[0] = jnp.zeros((channels, block), F32)
    step = 2 * block

    def mix(i, picked):
        start = pl.multiple_of(i * step, step)
        here_states = states_ref[:, :, pl.ds(start, step)]
        total = depth[0] * here_states[0].astype(F32)
        for j in range(1, state_count):
            total += depth[j] * here_states[j].astype(F32)
        mixed = total.astype(BF16)
        extended[2 * i + 1] = mixed[:, :block]
        extended[2 * i + 2] = mixed[:, block:]
        here = lax.broadcasted_iota(jnp.int32, (step, slots), 0) + start
        onehot = jnp.where(here == rows, 1.0, 0.0).astype(BF16)
        return picked + jnp.dot(
            here_states.reshape(state_count * channels, step), onehot, preferred_element_type=F32
        )

    steps = row_count // step
    states_copies[0].wait()
    picked = lax.fori_loop(
        0, steps // 2, mix, jnp.zeros((state_count * channels, slots), F32), unroll=MIX_UNROLL
    )
    states_copies[1].wait()
    picked = lax.fori_loop(steps // 2, steps, mix, picked, unroll=MIX_UNROLL)
    picked = picked.reshape(state_count, channels, slots)
    listed = depth[0] * picked[0]
    for j in range(1, state_count):
        listed += depth[j] * picked[j]
    listed = listed.astype(BF16)
    picked_states[...] = picked

    def widened(part):
        return jnp.concatenate([part] * per_block, axis=1)

    for p in range(vert):
        halo_send[p] = widened(listed[:, p * halo : (p + 1) * halo])

    pl.semaphore_wait(barrier, vert + feat - 2)
    halo_copies = vert_exchange(HALO_OUT, halo_send, halo_recv)
    cot_copies = [
        feat_copy(
            COT,
            k,
            cot_hbm.at[:, pl.ds(pl.multiple_of(feat_peer(k) * width, width), width)],
            cot_recv.at[my_feat],
        )
        for k in range(1, feat)
    ]
    bias_recv[my_feat] = jnp.broadcast_to(column_of(bias_ref[...]), (channels, block))
    bias_copies = [
        feat_copy(BIAS, k, bias_recv.at[my_feat], bias_recv.at[my_feat]) for k in range(1, feat)
    ]
    for copy in cot_copies + bias_copies:
        copy.start()
    halo_recv[my_vert] = halo_send[my_vert]
    plan_tiles(count_ref[0], dst_ref[...], src_ref[...], plan_vec, keep_vec)
    plan_copy = pltpu.make_async_copy(plan_vec, plan, local_sem.at[4])
    plan_copy.start()
    keep_copy = pltpu.make_async_copy(keep_vec, keep, local_sem.at[5])
    keep_copy.start()
    weight_copy.wait()
    own_cot.wait()
    weight = weight_ref[...]
    weight_t[...] = weight.astype(F32).T.astype(BF16)

    arrived(halo_copies)
    for j in range(src_blocks - row_blocks):
        extended[row_blocks + j + 1] = jnp.concatenate(
            [halo_recv[j * per_block + h, :, :halo] for h in range(per_block)], axis=1
        )
    for copy in tile_copies:
        copy.wait()

    plan_copy.wait()
    keep_copy.wait()

    def closing(row, n):
        return running[jnp.clip(plan[row, n], 0, running.shape[0] - 1)]

    def tile_pass(row, source, dims):
        def pick(k):
            word = plan[row, k]
            tile = tiles[jnp.minimum(lax.shift_right_logical(word, 7), capacity - 1)]
            own = jnp.minimum(lax.bitwise_and(word, STRIDE - 1), source.shape[0] - 1)
            return source[own], tile

        def group(g, total):
            products = []
            for u in range(GROUP):
                k = g * GROUP + u
                left, left_tile = pick(2 * k)
                right, right_tile = pick(2 * k + 1)
                products.append(
                    lax.dot_general(
                        jnp.concatenate([left, right], axis=1),
                        jnp.concatenate([left_tile, right_tile], axis=dims),
                        (((1,), (dims,)), ((), ())),
                        preferred_element_type=F32,
                    )
                )
            for u in range(GROUP):
                k = g * GROUP + u
                total = total * keep[row, 2 * k] + products[u]
                running[k + 1] = total
            return total

        lax.fori_loop(
            0,
            (running.shape[0] - 1) // GROUP,
            group,
            jnp.zeros((channels, block), F32),
            unroll=REPEAT,
        )

    tile_pass(0, extended, 1)
    for n in range(row_blocks):
        j = n % per_width
        agg_send[n // per_width, :, j * block : (j + 1) * block] = closing(1, n).astype(BF16)
    agg_copies = feat_exchange(AGG, agg_send, agg_recv)
    agg_recv[my_feat] = agg_send[my_feat]
    arrived(cot_copies)
    arrived(bias_copies)
    arrived(agg_copies)

    aggregated = agg_recv[...].reshape(features, width)
    bias = bias_recv[...].reshape(features, block)[:, :1]
    pre_act = jnp.dot(weight_t[...], aggregated, preferred_element_type=F32) + bias
    sigmoid_pre = jax.nn.sigmoid(pre_act)
    grad_pre32 = (
        cot_recv[...].reshape(features, width).astype(F32)
        * sigmoid_pre
        * (1.0 + pre_act * (1.0 - sigmoid_pre))
    )
    grad_pre = grad_pre32.astype(BF16)
    grad_send[...] = (
        jnp.dot(weight, grad_pre, preferred_element_type=F32)
        .astype(BF16)
        .reshape(feat, channels, width)
    )
    grad_copies = feat_exchange(GRAD, grad_send, grad_recv)
    grad_recv[my_feat] = grad_send[my_feat]
    layer_send[...] = (pre_act * sigmoid_pre).astype(BF16).reshape(feat, channels, width)
    layer_copies = feat_exchange(LAYER, layer_send, layer_recv)
    layer_recv[my_feat] = layer_send[my_feat]
    terms_send[:, :, :features] = lax.dot_general(
        aggregated, grad_pre, (((1,), (1,)), ((), ())), preferred_element_type=F32
    ).reshape(feat, channels, features)
    terms_send[:, :, features:] = jnp.broadcast_to(
        jnp.sum(grad_pre.astype(F32), axis=1, keepdims=True), (features, block)
    ).reshape(feat, channels, block)
    terms_copies = feat_exchange(TERMS, terms_send, terms_recv)
    terms_recv[my_feat] = terms_send[my_feat]

    grad_blocks[0] = jnp.zeros((channels, block), BF16)
    rows_col = jnp.broadcast_to(rows.astype(F32), (block, slots)).T[:, :1].astype(jnp.int32)

    arrived(grad_copies)
    for n in range(row_blocks):
        j = n % per_width
        grad_blocks[n + 1] = grad_recv[n // per_width, :, j * block : (j + 1) * block]
    tile_pass(2, grad_blocks, 0)

    for s in range(row_blocks, src_blocks):
        value = closing(3, s).astype(BF16)
        for h in range(per_block):
            back_send[(s - row_blocks) * per_block + h] = widened(
                value[:, h * halo : (h + 1) * halo]
            )
    back_copies = vert_exchange(HALO_BACK, back_send, back_recv)
    back_recv[my_vert] = back_send[my_vert]
    for s in range(row_blocks):
        mixed_grad[:, s * block : (s + 1) * block] = closing(3, s)

    def own_sums(i, sums):
        start = pl.multiple_of(i * step, step)
        own = mixed_grad[:, pl.ds(start, step)]
        out = []
        for j in range(state_count):
            term = states_ref[j, :, pl.ds(start, step)].astype(F32) * own
            out.append(sums[j] + term[:, :block] + term[:, block:])
        return tuple(out)

    sums = lax.fori_loop(
        0,
        steps,
        own_sums,
        tuple(jnp.zeros((channels, block), F32) for _ in range(state_count)),
        unroll=4,
    )
    own_depth = [jnp.sum(part, axis=1, keepdims=True) for part in sums]

    arrived(back_copies)
    returned = jnp.concatenate([back_recv[q, :, :halo] for q in range(vert)], axis=1)
    returned32 = returned.astype(F32)
    lane = lax.broadcasted_iota(jnp.int32, (channels, block), 1)
    packed = jnp.zeros((channels, block), F32)
    for j in range(state_count):
        listed_sum = jnp.sum(picked_states[j] * returned32, axis=1, keepdims=True)
        packed = jnp.where(lane == j, own_depth[j] + listed_sum, packed)
    depth_recv[my_vert] = packed
    depth_copies = vert_spread(DEPTH, depth_recv)

    arrived(terms_copies)
    total = terms_recv[0]
    for f in range(1, feat):
        total += terms_recv[f]
    sums_recv[my_vert] = total
    sums_copies = vert_spread(SUMS, sums_recv)

    def finish(i, carry):
        start = pl.multiple_of(i * step, step)
        here = lax.broadcasted_iota(jnp.int32, (slots, step), 1) + start
        onehot = jnp.where(here == rows_col, 1.0, 0.0).astype(BF16)
        mixed_grad[:, pl.ds(start, step)] += jnp.dot(
            returned, onehot, preferred_element_type=F32
        )
        return carry

    lax.fori_loop(0, steps, finish, 0, unroll=MIX_UNROLL)
    arrived(layer_copies)
    for f in range(feat):
        layer_ref[:, f * width : (f + 1) * width] = layer_recv[f]

    arrived(sums_copies)
    total = sums_recv[0]
    for q in range(1, vert):
        total += sums_recv[q]
    grad_weight_ref[...] = total[:, :features] * norm_scale
    grad_bias_ref[...] = row_of(total[:, features : features + 1] * norm_scale)
    arrived(depth_copies)
    total = depth_recv[0]
    for q in range(1, vert):
        total += depth_recv[q]
    for j in range(state_count):
        grad_depth_ref[j : j + 1, :] = row_of(total[:, j : j + 1] * norm_scale)
    for copies in (
        halo_copies,
        cot_copies,
        bias_copies,
        agg_copies,
        grad_copies,
        layer_copies,
        terms_copies,
        back_copies,
        sums_copies,
        depth_copies,
    ):
        for copy in copies:
            copy.wait_send()


def output_kernel(
    layer, mixed_grad, grad_weight, grad_bias, grad_depth, depth_ref, layer_out, states_out, *outs
):
    layer_out[...] = layer[...]
    for ref, out in zip((grad_weight, grad_bias, grad_depth), outs):
        out[...] = ref[...]
    for j in range(depth_ref.shape[0]):
        scale = column_of(depth_ref[j : j + 1, :])
        states_out[j] = (scale * mixed_grad[...]).astype(BF16)


def local(
    states,
    depth_weight,
    tile_values,
    tile_dst,
    tile_src,
    tile_count,
    send_rows,
    weight,
    bias_vec,
    cotangent,
):
    state_count, channels, row_count = states.shape
    capacity, block = tile_values.shape[1], tile_values.shape[2]
    vert, feat = lax.axis_size("vert"), lax.axis_size("feat")
    halo = send_rows.shape[2]
    slots = send_rows.shape[1] * halo
    width = row_count // feat
    features = channels * feat
    row_blocks = row_count // block
    src_blocks = (row_count + slots) // block
    norm_scale = 1.0 / math.sqrt(vert * row_count)

    vmem = pl.BlockSpec(memory_space=pltpu.VMEM)
    smem = pl.BlockSpec(memory_space=pltpu.SMEM)
    most = max(vert, feat)
    terms = features + block
    hbm = pl.BlockSpec(memory_space=pltpu.HBM)
    pairs = -(-((capacity + src_blocks) // 2) // GROUP) * GROUP
    lanes = -(-2 * pairs // block) * block
    layer, mixed_grad, grad_weight, grad_bias, grad_depth = pl.pallas_call(
        functools.partial(
            whole_kernel, (vert, feat, channels, row_count, block, halo), norm_scale
        ),
        out_shape=(
            jax.ShapeDtypeStruct((channels, row_count), BF16),
            jax.ShapeDtypeStruct((channels, row_count), F32),
            jax.ShapeDtypeStruct((channels, features), F32),
            jax.ShapeDtypeStruct((1, channels), F32),
            jax.ShapeDtypeStruct((state_count, channels), F32),
        ),
        in_specs=[smem] + [vmem] * 4 + [hbm, vmem] + [hbm] * 3,
        out_specs=(vmem,) * 5,
        scratch_shapes=[
            pltpu.VMEM((capacity, block, block), BF16),
            pltpu.VMEM((src_blocks + 1, channels, block), BF16),
            pltpu.VMEM((pairs + 1, channels, block), F32),
            pltpu.VMEM((vert, channels, block), BF16),
            pltpu.VMEM((vert, channels, block), BF16),
            pltpu.VMEM((vert, channels, block), BF16),
            pltpu.VMEM((vert, channels, block), BF16),
            pltpu.VMEM((feat, channels, width), BF16),
            pltpu.VMEM((feat, channels, block), F32),
            pltpu.VMEM((feat, channels, width), BF16),
            pltpu.VMEM((feat, channels, width), BF16),
            pltpu.VMEM((feat, channels, width), BF16),
            pltpu.VMEM((feat, channels, width), BF16),
            pltpu.VMEM((feat, channels, width), BF16),
            pltpu.VMEM((feat, channels, width), BF16),
            pltpu.VMEM((feat, channels, terms), F32),
            pltpu.VMEM((feat, channels, terms), F32),
            pltpu.VMEM((vert, channels, terms), F32),
            pltpu.VMEM((vert, channels, block), F32),
            pltpu.VMEM((row_blocks + 1, channels, block), BF16),
            pltpu.VMEM((features, features), BF16),
            pltpu.VMEM((features, features), BF16),
            pltpu.VMEM((state_count, channels, row_count), BF16),
            pltpu.VMEM((8, lanes), jnp.int32),
            pltpu.SMEM((8, lanes), jnp.int32),
            pltpu.VMEM((8, lanes), F32),
            pltpu.SMEM((8, lanes), F32),
            pltpu.VMEM((state_count, channels, slots), F32),
            pltpu.SemaphoreType.DMA((TILE_PARTS,)),
            pltpu.SemaphoreType.DMA((6,)),
            pltpu.SemaphoreType.DMA((10, most)),
            pltpu.SemaphoreType.DMA((10, most)),
        ],
        compiler_params=pltpu.CompilerParams(
            collective_id=0, has_side_effects=True, vmem_limit_bytes=VMEM_LIMIT
        ),
    )(
        tile_count,
        tile_dst,
        tile_src,
        depth_weight,
        send_rows,
        weight,
        bias_vec[None, :],
        states,
        cotangent,
        tile_values,
    )
    layer_out, grad_states, grad_weight, grad_bias, grad_depth = pl.pallas_call(
        output_kernel,
        out_shape=(
            jax.ShapeDtypeStruct((channels, row_count), BF16),
            jax.ShapeDtypeStruct((state_count, channels, row_count), BF16),
            jax.ShapeDtypeStruct((channels, features), F32),
            jax.ShapeDtypeStruct((1, channels), F32),
            jax.ShapeDtypeStruct((state_count, channels), F32),
        ),
        in_specs=[vmem] * 6,
        out_specs=(vmem,) * 5,
        compiler_params=pltpu.CompilerParams(vmem_limit_bytes=VMEM_LIMIT),
    )(layer, mixed_grad, grad_weight, grad_bias, grad_depth, depth_weight)
    return layer_out, grad_states, grad_weight, grad_bias[0], grad_depth


def solution(mesh):
    placed = (
        P(None, "feat", "vert"),
        P(None, "feat"),
        P("vert", None, None, None),
        P("vert", None),
        P("vert", None),
        P("vert"),
        P("vert", None, None),
        P(),
        P("feat"),
        P("feat", "vert"),
    )
    return jax.shard_map(
        local,
        mesh=mesh,
        in_specs=placed,
        out_specs=(
            P("feat", "vert"),
            P(None, "feat", "vert"),
            P("feat", None),
            P("feat"),
            P(None, "feat"),
        ),
        check_vma=False,
    )
```

```python
import functools
import math

import jax
import jax.numpy as jnp
from jax import lax
from jax.experimental import pallas as pl
from jax.experimental.pallas import tpu as pltpu
from jax.sharding import PartitionSpec as P

F32 = jnp.float32
BF16 = jnp.bfloat16
HALO_OUT, COT, BIAS, AGG, GRAD, LAYER, TERMS, HALO_BACK, SUMS, DEPTH = range(10)
TILE_PARTS = 8
GROUP = 10
REPEAT = 3
VMEM_LIMIT = 63 * 1024 * 1024
STRIDE = 128
MIX_UNROLL = 8


def diagonal(size):
    down = lax.broadcasted_iota(jnp.int32, (size, size), 0)
    return down == lax.broadcasted_iota(jnp.int32, (size, size), 1)


def column_of(row):
    size = row.shape[1]
    spread = jnp.broadcast_to(row, (size, size))
    return jnp.sum(jnp.where(diagonal(size), spread, 0.0), axis=1, keepdims=True)


def row_of(column):
    size = column.shape[0]
    spread = jnp.broadcast_to(column, (size, size))
    return jnp.sum(jnp.where(diagonal(size), spread, 0.0), axis=0, keepdims=True)


def plan_tiles(tile_total, dst, src, plan_vec, keep_vec):
    capacity = dst.shape[1]
    lanes = plan_vec.shape[1]
    live = lax.broadcasted_iota(jnp.int32, (1, capacity), 1) < tile_total
    dead = float(STRIDE - 1)
    dst, src = dst.astype(F32), src.astype(F32)
    dst_key, src_key = jnp.where(live, dst, dead), jnp.where(live, src, dead)
    down = lax.broadcasted_iota(jnp.int32, (STRIDE, capacity), 0)
    stacked = jnp.where(down == 0, dst_key, jnp.where(down == 1, src_key, 0.0))
    stacked = jnp.where(down == 2, dst, jnp.where(down == 3, src, stacked))
    turned = stacked.T
    square = (capacity, capacity)
    earlier = lax.broadcasted_iota(jnp.int32, square, 1) < lax.broadcasted_iota(
        jnp.int32, square, 0
    )
    place = lax.broadcasted_iota(jnp.int32, (capacity, 1), 0).astype(F32)
    bins = lax.broadcasted_iota(jnp.int32, (capacity, STRIDE), 1).astype(F32)
    spots = lax.broadcasted_iota(jnp.int32, (capacity, lanes), 1).astype(F32)
    plan_vec[...] = jnp.zeros(plan_vec.shape, jnp.int32)
    keep_vec[...] = jnp.zeros(keep_vec.shape, F32)
    for row, key_row, key, other in (
        (0, dst_key, turned[:, 0:1], turned[:, 3:4]),
        (2, src_key, turned[:, 1:2], turned[:, 2:3]),
    ):
        same = jnp.where((key_row == key) & earlier, 1.0, 0.0)
        inside = jnp.sum(same, axis=1, keepdims=True)
        counts = jnp.sum(jnp.where(bins == key, 1.0, 0.0), axis=0, keepdims=True)
        pairs = jnp.floor((counts + 1.0) * 0.5)
        first = jnp.sum(jnp.where(bins < key, pairs, 0.0), axis=1, keepdims=True)
        spot = jnp.where(key == dead, -1.0, 2.0 * first + inside)
        word = place * STRIDE + other + 1.0
        goes_on = jnp.where(inside > 0.0, 1.0, 0.0)
        keep_vec[row : row + 1, :] = jnp.sum(
            jnp.where(spots == spot, goes_on, 0.0), axis=0, keepdims=True
        )
        words = jnp.sum(jnp.where(spots == spot, word, 0.0), axis=0, keepdims=True)
        plan_vec[row : row + 1, :] = words.astype(jnp.int32)
        after = jnp.floor(spot * 0.5) + 1.0
        last = jnp.max(jnp.where(bins == key, after, 0.0), axis=0, keepdims=True)
        plan_vec[row + 1 : row + 2, :STRIDE] = last.astype(jnp.int32)


def whole_kernel(
    sizes,
    norm_scale,
    count_ref,
    dst_ref,
    src_ref,
    depth_ref,
    rows_ref,
    weight_hbm,
    bias_ref,
    states_hbm,
    cot_hbm,
    tiles_hbm,
    layer_ref,
    mixed_grad,
    grad_weight_ref,
    grad_bias_ref,
    grad_depth_ref,
    tiles,
    extended,
    running,
    halo_send,
    halo_recv,
    back_send,
    back_recv,
    cot_recv,
    bias_recv,
    agg_send,
    agg_recv,
    grad_send,
    grad_recv,
    layer_send,
    layer_recv,
    terms_send,
    terms_recv,
    sums_recv,
    depth_recv,
    grad_blocks,
    weight_t,
    weight_ref,
    states_ref,
    plan_vec,
    plan,
    keep_vec,
    keep,
    picked_states,
    tile_sem,
    local_sem,
    send_sem,
    recv_sem,
):
    vert, feat, channels, row_count, block, halo = sizes
    state_count = states_ref.shape[0]
    capacity = tiles.shape[0]
    width = row_count // feat
    features = channels * feat
    row_blocks = row_count // block
    src_blocks = extended.shape[0] - 1
    slots = vert * halo
    per_block = block // halo
    per_width = width // block
    my_vert = lax.axis_index("vert")
    my_feat = lax.axis_index("feat")

    def vert_peer(k):
        return lax.rem(my_vert + k, vert)

    def feat_peer(k):
        return lax.rem(my_feat + k, feat)

    def vert_copy(kind, k, src, dst):
        return pltpu.make_async_remote_copy(
            src_ref=src,
            dst_ref=dst,
            send_sem=send_sem.at[kind, k],
            recv_sem=recv_sem.at[kind, k],
            device_id=(vert_peer(k), my_feat),
            device_id_type=pl.DeviceIdType.MESH,
        )

    def feat_copy(kind, k, src, dst):
        return pltpu.make_async_remote_copy(
            src_ref=src,
            dst_ref=dst,
            send_sem=send_sem.at[kind, k],
            recv_sem=recv_sem.at[kind, k],
            device_id=(my_vert, feat_peer(k)),
            device_id_type=pl.DeviceIdType.MESH,
        )

    def vert_exchange(kind, send, recv):
        copies = [
            vert_copy(kind, k, send.at[vert_peer(k)], recv.at[my_vert]) for k in range(1, vert)
        ]
        for copy in copies:
            copy.start()
        return copies

    def vert_spread(kind, recv):
        copies = [
            vert_copy(kind, k, recv.at[my_vert], recv.at[my_vert]) for k in range(1, vert)
        ]
        for copy in copies:
            copy.start()
        return copies

    def feat_exchange(kind, send, recv):
        copies = [
            feat_copy(kind, k, send.at[feat_peer(k)], recv.at[my_feat]) for k in range(1, feat)
        ]
        for copy in copies:
            copy.start()
        return copies

    def arrived(copies):
        for copy in copies:
            copy.wait_recv()

    barrier = pltpu.get_barrier_semaphore()
    for k in range(1, vert):
        pl.semaphore_signal(
            barrier, inc=1, device_id=(vert_peer(k), my_feat), device_id_type=pl.DeviceIdType.MESH
        )
    for k in range(1, feat):
        pl.semaphore_signal(
            barrier, inc=1, device_id=(my_vert, feat_peer(k)), device_id_type=pl.DeviceIdType.MESH
        )

    half = row_count // 2
    states_copies = [
        pltpu.make_async_copy(
            states_hbm.at[:, :, pl.ds(i * half, half)],
            states_ref.at[:, :, pl.ds(i * half, half)],
            local_sem.at[i],
        )
        for i in range(2)
    ]
    weight_copy = pltpu.make_async_copy(weight_hbm, weight_ref, local_sem.at[2])
    own_cot = pltpu.make_async_copy(
        cot_hbm.at[:, pl.ds(pl.multiple_of(my_feat * width, width), width)],
        cot_recv.at[my_feat],
        local_sem.at[3],
    )
    for copy in states_copies + [weight_copy, own_cot]:
        copy.start()
    part = capacity // TILE_PARTS
    tile_copies = [
        pltpu.make_async_copy(
            tiles_hbm.at[0, pl.ds(i * part, part)], tiles.at[pl.ds(i * part, part)], tile_sem.at[i]
        )
        for i in range(TILE_PARTS)
    ]
    for copy in tile_copies:
        copy.start()

    depth = [column_of(depth_ref[j : j + 1, :]) for j in range(state_count)]
    rows = jnp.concatenate([rows_ref[0, p : p + 1, :] for p in range(vert)], axis=1)
    extended[0] = jnp.zeros((channels, block), BF16)
    running[0] = jnp.zeros((channels, block), F32)
    step = 2 * block

    def mix(i, picked):
        start = pl.multiple_of(i * step, step)
        here_states = states_ref[:, :, pl.ds(start, step)]
        total = depth[0] * here_states[0].astype(F32)
        for j in range(1, state_count):
            total += depth[j] * here_states[j].astype(F32)
        mixed = total.astype(BF16)
        extended[2 * i + 1] = mixed[:, :block]
        extended[2 * i + 2] = mixed[:, block:]
        here = lax.broadcasted_iota(jnp.int32, (step, slots), 0) + start
        onehot = jnp.where(here == rows, 1.0, 0.0).astype(BF16)
        return picked + jnp.dot(
            here_states.reshape(state_count * channels, step), onehot, preferred_element_type=F32
        )

    steps = row_count // step
    states_copies[0].wait()
    picked = lax.fori_loop(
        0, steps // 2, mix, jnp.zeros((state_count * channels, slots), F32), unroll=MIX_UNROLL
    )
    states_copies[1].wait()
    picked = lax.fori_loop(steps // 2, steps, mix, picked, unroll=MIX_UNROLL)
    picked = picked.reshape(state_count, channels, slots)
    listed = depth[0] * picked[0]
    for j in range(1, state_count):
        listed += depth[j] * picked[j]
    listed = listed.astype(BF16)
    picked_states[...] = picked

    def widened(part):
        return jnp.concatenate([part] * per_block, axis=1)

    for p in range(vert):
        halo_send[p] = widened(listed[:, p * halo : (p + 1) * halo])

    pl.semaphore_wait(barrier, vert + feat - 2)
    halo_copies = vert_exchange(HALO_OUT, halo_send, halo_recv)
    cot_copies = [
        feat_copy(
            COT,
            k,
            cot_hbm.at[:, pl.ds(pl.multiple_of(feat_peer(k) * width, width), width)],
            cot_recv.at[my_feat],
        )
        for k in range(1, feat)
    ]
    bias_recv[my_feat] = jnp.broadcast_to(column_of(bias_ref[...]), (channels, block))
    bias_copies = [
        feat_copy(BIAS, k, bias_recv.at[my_feat], bias_recv.at[my_feat]) for k in range(1, feat)
    ]
    for copy in cot_copies + bias_copies:
        copy.start()
    halo_recv[my_vert] = halo_send[my_vert]
    plan_tiles(count_ref[0], dst_ref[...], src_ref[...], plan_vec, keep_vec)
    plan_copy = pltpu.make_async_copy(plan_vec, plan, local_sem.at[4])
    plan_copy.start()
    keep_copy = pltpu.make_async_copy(keep_vec, keep, local_sem.at[5])
    keep_copy.start()
    weight_copy.wait()
    own_cot.wait()
    weight = weight_ref[...]
    weight_t[...] = weight.astype(F32).T.astype(BF16)

    arrived(halo_copies)
    for j in range(src_blocks - row_blocks):
        extended[row_blocks + j + 1] = jnp.concatenate(
            [halo_recv[j * per_block + h, :, :halo] for h in range(per_block)], axis=1
        )
    for copy in tile_copies:
        copy.wait()

    plan_copy.wait()
    keep_copy.wait()

    def closing(row, n):
        return running[jnp.clip(plan[row, n], 0, running.shape[0] - 1)]

    def tile_pass(row, source, dims):
        def pick(k):
            word = plan[row, k]
            tile = tiles[jnp.minimum(lax.shift_right_logical(word, 7), capacity - 1)]
            own = jnp.minimum(lax.bitwise_and(word, STRIDE - 1), source.shape[0] - 1)
            return source[own], tile

        def group(g, total):
            products = []
            for u in range(0, GROUP, 2):
                k = 2 * (g * GROUP + u)
                sources, parts = zip(*[pick(k + i) for i in range(4)])
                rows_now = jnp.concatenate(
                    [
                        jnp.concatenate(sources[:2], axis=1),
                        jnp.concatenate(sources[2:], axis=1),
                    ],
                    axis=0,
                )
                tiles_now = jnp.concatenate(
                    [
                        jnp.concatenate(parts[:2], axis=dims),
                        jnp.concatenate(parts[2:], axis=dims),
                    ],
                    axis=1 - dims,
                )
                product = lax.dot_general(
                    rows_now,
                    tiles_now,
                    (((1,), (dims,)), ((), ())),
                    preferred_element_type=F32,
                )
                products.append(product[:channels, :block])
                products.append(product[channels:, block:])
            for u in range(GROUP):
                k = g * GROUP + u
                total = total * keep[row, 2 * k] + products[u]
                running[k + 1] = total
            return total

        lax.fori_loop(
            0,
            (running.shape[0] - 1) // GROUP,
            group,
            jnp.zeros((channels, block), F32),
            unroll=REPEAT,
        )

    tile_pass(0, extended, 1)
    for n in range(row_blocks):
        j = n % per_width
        agg_send[n // per_width, :, j * block : (j + 1) * block] = closing(1, n).astype(BF16)
    agg_copies = feat_exchange(AGG, agg_send, agg_recv)
    agg_recv[my_feat] = agg_send[my_feat]
    arrived(cot_copies)
    arrived(bias_copies)
    arrived(agg_copies)

    aggregated = agg_recv[...].reshape(features, width)
    bias = bias_recv[...].reshape(features, block)[:, :1]
    pre_act = jnp.dot(weight_t[...], aggregated, preferred_element_type=F32) + bias
    sigmoid_pre = jax.nn.sigmoid(pre_act)
    grad_pre32 = (
        cot_recv[...].reshape(features, width).astype(F32)
        * sigmoid_pre
        * (1.0 + pre_act * (1.0 - sigmoid_pre))
    )
    grad_pre = grad_pre32.astype(BF16)
    grad_send[...] = (
        jnp.dot(weight, grad_pre, preferred_element_type=F32)
        .astype(BF16)
        .reshape(feat, channels, width)
    )
    grad_copies = feat_exchange(GRAD, grad_send, grad_recv)
    grad_recv[my_feat] = grad_send[my_feat]
    layer_send[...] = (pre_act * sigmoid_pre).astype(BF16).reshape(feat, channels, width)
    layer_copies = feat_exchange(LAYER, layer_send, layer_recv)
    layer_recv[my_feat] = layer_send[my_feat]
    terms_send[:, :, :features] = lax.dot_general(
        aggregated, grad_pre, (((1,), (1,)), ((), ())), preferred_element_type=F32
    ).reshape(feat, channels, features)
    terms_send[:, :, features:] = jnp.broadcast_to(
        jnp.sum(grad_pre.astype(F32), axis=1, keepdims=True), (features, block)
    ).reshape(feat, channels, block)
    terms_copies = feat_exchange(TERMS, terms_send, terms_recv)
    terms_recv[my_feat] = terms_send[my_feat]

    grad_blocks[0] = jnp.zeros((channels, block), BF16)
    rows_col = jnp.broadcast_to(rows.astype(F32), (block, slots)).T[:, :1].astype(jnp.int32)

    arrived(grad_copies)
    for n in range(row_blocks):
        j = n % per_width
        grad_blocks[n + 1] = grad_recv[n // per_width, :, j * block : (j + 1) * block]
    tile_pass(2, grad_blocks, 0)

    for s in range(row_blocks, src_blocks):
        value = closing(3, s).astype(BF16)
        for h in range(per_block):
            back_send[(s - row_blocks) * per_block + h] = widened(
                value[:, h * halo : (h + 1) * halo]
            )
    back_copies = vert_exchange(HALO_BACK, back_send, back_recv)
    back_recv[my_vert] = back_send[my_vert]
    for s in range(row_blocks):
        mixed_grad[:, s * block : (s + 1) * block] = closing(3, s)

    arrived(terms_copies)
    total = terms_recv[0]
    for f in range(1, feat):
        total += terms_recv[f]
    sums_recv[my_vert] = total
    sums_copies = vert_spread(SUMS, sums_recv)

    def own_sums(i, sums):
        start = pl.multiple_of(i * step, step)
        own = mixed_grad[:, pl.ds(start, step)]
        out = []
        for j in range(state_count):
            term = states_ref[j, :, pl.ds(start, step)].astype(F32) * own
            out.append(sums[j] + term[:, :block] + term[:, block:])
        return tuple(out)

    sums = lax.fori_loop(
        0,
        steps,
        own_sums,
        tuple(jnp.zeros((channels, block), F32) for _ in range(state_count)),
        unroll=4,
    )
    own_depth = [jnp.sum(part, axis=1, keepdims=True) for part in sums]

    arrived(back_copies)
    returned = jnp.concatenate([back_recv[q, :, :halo] for q in range(vert)], axis=1)
    returned32 = returned.astype(F32)
    lane = lax.broadcasted_iota(jnp.int32, (channels, block), 1)
    packed = jnp.zeros((channels, block), F32)
    for j in range(state_count):
        listed_sum = jnp.sum(picked_states[j] * returned32, axis=1, keepdims=True)
        packed = jnp.where(lane == j, own_depth[j] + listed_sum, packed)
    depth_recv[my_vert] = packed
    depth_copies = vert_spread(DEPTH, depth_recv)

    def finish(i, carry):
        start = pl.multiple_of(i * step, step)
        here = lax.broadcasted_iota(jnp.int32, (slots, step), 1) + start
        onehot = jnp.where(here == rows_col, 1.0, 0.0).astype(BF16)
        mixed_grad[:, pl.ds(start, step)] += jnp.dot(
            returned, onehot, preferred_element_type=F32
        )
        return carry

    lax.fori_loop(0, steps, finish, 0, unroll=MIX_UNROLL)
    arrived(layer_copies)
    for f in range(feat):
        layer_ref[:, f * width : (f + 1) * width] = layer_recv[f]

    arrived(sums_copies)
    total = sums_recv[0]
    for q in range(1, vert):
        total += sums_recv[q]
    grad_weight_ref[...] = total[:, :features] * norm_scale
    grad_bias_ref[...] = row_of(total[:, features : features + 1] * norm_scale)
    arrived(depth_copies)
    total = depth_recv[0]
    for q in range(1, vert):
        total += depth_recv[q]
    for j in range(state_count):
        grad_depth_ref[j : j + 1, :] = row_of(total[:, j : j + 1] * norm_scale)
    for copies in (
        halo_copies,
        cot_copies,
        bias_copies,
        agg_copies,
        grad_copies,
        layer_copies,
        terms_copies,
        back_copies,
        sums_copies,
        depth_copies,
    ):
        for copy in copies:
            copy.wait_send()


def output_kernel(
    layer, mixed_grad, grad_weight, grad_bias, grad_depth, depth_ref, layer_out, states_out, *outs
):
    layer_out[...] = layer[...]
    for ref, out in zip((grad_weight, grad_bias, grad_depth), outs):
        out[...] = ref[...]
    for j in range(depth_ref.shape[0]):
        scale = column_of(depth_ref[j : j + 1, :])
        states_out[j] = (scale * mixed_grad[...]).astype(BF16)


def local(
    states,
    depth_weight,
    tile_values,
    tile_dst,
    tile_src,
    tile_count,
    send_rows,
    weight,
    bias_vec,
    cotangent,
):
    state_count, channels, row_count = states.shape
    capacity, block = tile_values.shape[1], tile_values.shape[2]
    vert, feat = lax.axis_size("vert"), lax.axis_size("feat")
    halo = send_rows.shape[2]
    slots = send_rows.shape[1] * halo
    width = row_count // feat
    features = channels * feat
    row_blocks = row_count // block
    src_blocks = (row_count + slots) // block
    norm_scale = 1.0 / math.sqrt(vert * row_count)

    vmem = pl.BlockSpec(memory_space=pltpu.VMEM)
    smem = pl.BlockSpec(memory_space=pltpu.SMEM)
    most = max(vert, feat)
    terms = features + block
    hbm = pl.BlockSpec(memory_space=pltpu.HBM)
    pairs = -(-((capacity + src_blocks) // 2) // GROUP) * GROUP
    lanes = -(-2 * pairs // block) * block
    layer, mixed_grad, grad_weight, grad_bias, grad_depth = pl.pallas_call(
        functools.partial(
            whole_kernel, (vert, feat, channels, row_count, block, halo), norm_scale
        ),
        out_shape=(
            jax.ShapeDtypeStruct((channels, row_count), BF16),
            jax.ShapeDtypeStruct((channels, row_count), F32),
            jax.ShapeDtypeStruct((channels, features), F32),
            jax.ShapeDtypeStruct((1, channels), F32),
            jax.ShapeDtypeStruct((state_count, channels), F32),
        ),
        in_specs=[smem] + [vmem] * 4 + [hbm, vmem] + [hbm] * 3,
        out_specs=(vmem,) * 5,
        scratch_shapes=[
            pltpu.VMEM((capacity, block, block), BF16),
            pltpu.VMEM((src_blocks + 1, channels, block), BF16),
            pltpu.VMEM((pairs + 1, channels, block), F32),
            pltpu.VMEM((vert, channels, block), BF16),
            pltpu.VMEM((vert, channels, block), BF16),
            pltpu.VMEM((vert, channels, block), BF16),
            pltpu.VMEM((vert, channels, block), BF16),
            pltpu.VMEM((feat, channels, width), BF16),
            pltpu.VMEM((feat, channels, block), F32),
            pltpu.VMEM((feat, channels, width), BF16),
            pltpu.VMEM((feat, channels, width), BF16),
            pltpu.VMEM((feat, channels, width), BF16),
            pltpu.VMEM((feat, channels, width), BF16),
            pltpu.VMEM((feat, channels, width), BF16),
            pltpu.VMEM((feat, channels, width), BF16),
            pltpu.VMEM((feat, channels, terms), F32),
            pltpu.VMEM((feat, channels, terms), F32),
            pltpu.VMEM((vert, channels, terms), F32),
            pltpu.VMEM((vert, channels, block), F32),
            pltpu.VMEM((row_blocks + 1, channels, block), BF16),
            pltpu.VMEM((features, features), BF16),
            pltpu.VMEM((features, features), BF16),
            pltpu.VMEM((state_count, channels, row_count), BF16),
            pltpu.VMEM((8, lanes), jnp.int32),
            pltpu.SMEM((8, lanes), jnp.int32),
            pltpu.VMEM((8, lanes), F32),
            pltpu.SMEM((8, lanes), F32),
            pltpu.VMEM((state_count, channels, slots), F32),
            pltpu.SemaphoreType.DMA((TILE_PARTS,)),
            pltpu.SemaphoreType.DMA((6,)),
            pltpu.SemaphoreType.DMA((10, most)),
            pltpu.SemaphoreType.DMA((10, most)),
        ],
        compiler_params=pltpu.CompilerParams(
            collective_id=0, has_side_effects=True, vmem_limit_bytes=VMEM_LIMIT
        ),
    )(
        tile_count,
        tile_dst,
        tile_src,
        depth_weight,
        send_rows,
        weight,
        bias_vec[None, :],
        states,
        cotangent,
        tile_values,
    )
    layer_out, grad_states, grad_weight, grad_bias, grad_depth = pl.pallas_call(
        output_kernel,
        out_shape=(
            jax.ShapeDtypeStruct((channels, row_count), BF16),
            jax.ShapeDtypeStruct((state_count, channels, row_count), BF16),
            jax.ShapeDtypeStruct((channels, features), F32),
            jax.ShapeDtypeStruct((1, channels), F32),
            jax.ShapeDtypeStruct((state_count, channels), F32),
        ),
        in_specs=[vmem] * 6,
        out_specs=(vmem,) * 5,
        compiler_params=pltpu.CompilerParams(vmem_limit_bytes=VMEM_LIMIT),
    )(layer, mixed_grad, grad_weight, grad_bias, grad_depth, depth_weight)
    return layer_out, grad_states, grad_weight, grad_bias[0], grad_depth


def solution(mesh):
    placed = (
        P(None, "feat", "vert"),
        P(None, "feat"),
        P("vert", None, None, None),
        P("vert", None),
        P("vert", None),
        P("vert"),
        P("vert", None, None),
        P(),
        P("feat"),
        P("feat", "vert"),
    )
    return jax.shard_map(
        local,
        mesh=mesh,
        in_specs=placed,
        out_specs=(
            P("feat", "vert"),
            P(None, "feat", "vert"),
            P("feat", None),
            P("feat"),
            P(None, "feat"),
        ),
        check_vma=False,
    )
```

```python
import functools
import math

import jax
import jax.numpy as jnp
from jax import lax
from jax.experimental import pallas as pl
from jax.experimental.pallas import tpu as pltpu
from jax.sharding import PartitionSpec as P

F32 = jnp.float32
BF16 = jnp.bfloat16
HALO_OUT, COT, BIAS, LAYER, TERMS, HALO_BACK, SUMS, DEPTH, AGG, AGG_B, GRAD, GRAD_B = range(12)
TILE_PARTS = 8
GROUP = 10
REPEAT = 3
VMEM_LIMIT = 63 * 1024 * 1024
STRIDE = 128
MIX_UNROLL = 8


def diagonal(size):
    down = lax.broadcasted_iota(jnp.int32, (size, size), 0)
    return down == lax.broadcasted_iota(jnp.int32, (size, size), 1)


def column_of(row):
    size = row.shape[1]
    spread = jnp.broadcast_to(row, (size, size))
    return jnp.sum(jnp.where(diagonal(size), spread, 0.0), axis=1, keepdims=True)


def row_of(column):
    size = column.shape[0]
    spread = jnp.broadcast_to(column, (size, size))
    return jnp.sum(jnp.where(diagonal(size), spread, 0.0), axis=0, keepdims=True)


def plan_tiles(tile_total, dst, src, plan_vec, keep_vec):
    capacity = dst.shape[1]
    lanes = plan_vec.shape[1]
    live = lax.broadcasted_iota(jnp.int32, (1, capacity), 1) < tile_total
    dead = float(STRIDE - 1)
    dst, src = dst.astype(F32), src.astype(F32)
    dst_key, src_key = jnp.where(live, dst, dead), jnp.where(live, src, dead)
    down = lax.broadcasted_iota(jnp.int32, (STRIDE, capacity), 0)
    stacked = jnp.where(down == 0, dst_key, jnp.where(down == 1, src_key, 0.0))
    stacked = jnp.where(down == 2, dst, jnp.where(down == 3, src, stacked))
    turned = stacked.T
    square = (capacity, capacity)
    earlier = lax.broadcasted_iota(jnp.int32, square, 1) < lax.broadcasted_iota(
        jnp.int32, square, 0
    )
    place = lax.broadcasted_iota(jnp.int32, (capacity, 1), 0).astype(F32)
    bins = lax.broadcasted_iota(jnp.int32, (capacity, STRIDE), 1).astype(F32)
    spots = lax.broadcasted_iota(jnp.int32, (capacity, lanes), 1).astype(F32)
    plan_vec[...] = jnp.zeros(plan_vec.shape, jnp.int32)
    keep_vec[...] = jnp.zeros(keep_vec.shape, F32)
    for row, key_row, key, other in (
        (0, dst_key, turned[:, 0:1], turned[:, 3:4]),
        (2, src_key, turned[:, 1:2], turned[:, 2:3]),
    ):
        same = jnp.where((key_row == key) & earlier, 1.0, 0.0)
        inside = jnp.sum(same, axis=1, keepdims=True)
        counts = jnp.sum(jnp.where(bins == key, 1.0, 0.0), axis=0, keepdims=True)
        pairs = jnp.floor((counts + 1.0) * 0.5)
        first = jnp.sum(jnp.where(bins < key, pairs, 0.0), axis=1, keepdims=True)
        spot = jnp.where(key == dead, -1.0, 2.0 * first + inside)
        word = place * STRIDE + other + 1.0
        goes_on = jnp.where(inside > 0.0, 1.0, 0.0)
        keep_vec[row : row + 1, :] = jnp.sum(
            jnp.where(spots == spot, goes_on, 0.0), axis=0, keepdims=True
        )
        words = jnp.sum(jnp.where(spots == spot, word, 0.0), axis=0, keepdims=True)
        plan_vec[row : row + 1, :] = words.astype(jnp.int32)
        after = jnp.floor(spot * 0.5) + 1.0
        last = jnp.max(jnp.where(bins == key, after, 0.0), axis=0, keepdims=True)
        plan_vec[row + 1 : row + 2, :STRIDE] = last.astype(jnp.int32)


def whole_kernel(
    sizes,
    norm_scale,
    count_ref,
    dst_ref,
    src_ref,
    depth_ref,
    rows_ref,
    weight_hbm,
    bias_ref,
    states_hbm,
    cot_hbm,
    tiles_hbm,
    layer_ref,
    mixed_grad,
    grad_weight_ref,
    grad_bias_ref,
    grad_depth_ref,
    tiles,
    extended,
    running,
    halo_send,
    halo_recv,
    back_send,
    back_recv,
    cot_recv,
    bias_recv,
    agg_send,
    agg_recv,
    grad_send,
    grad_recv,
    layer_send,
    layer_recv,
    terms_send,
    terms_recv,
    sums_recv,
    depth_recv,
    grad_blocks,
    weight_t,
    weight_ref,
    states_ref,
    plan_vec,
    plan,
    keep_vec,
    keep,
    picked_states,
    tile_sem,
    local_sem,
    send_sem,
    recv_sem,
):
    vert, feat, channels, row_count, block, halo = sizes
    state_count = states_ref.shape[0]
    capacity = tiles.shape[0]
    width = row_count // feat
    features = channels * feat
    row_blocks = row_count // block
    src_blocks = extended.shape[0] - 1
    slots = vert * halo
    per_block = block // halo
    per_width = width // block
    parts, part_width = agg_send.shape[0], agg_send.shape[3]
    per_part = part_width // block

    def spot_of(n):
        j = n % per_width
        start = (j % per_part) * block
        return j // per_part, n // per_width, slice(start, start + block)

    my_vert = lax.axis_index("vert")
    my_feat = lax.axis_index("feat")

    def vert_peer(k):
        return lax.rem(my_vert + k, vert)

    def feat_peer(k):
        return lax.rem(my_feat + k, feat)

    def vert_copy(kind, k, src, dst):
        return pltpu.make_async_remote_copy(
            src_ref=src,
            dst_ref=dst,
            send_sem=send_sem.at[kind, k],
            recv_sem=recv_sem.at[kind, k],
            device_id=(vert_peer(k), my_feat),
            device_id_type=pl.DeviceIdType.MESH,
        )

    def feat_copy(kind, k, src, dst):
        return pltpu.make_async_remote_copy(
            src_ref=src,
            dst_ref=dst,
            send_sem=send_sem.at[kind, k],
            recv_sem=recv_sem.at[kind, k],
            device_id=(my_vert, feat_peer(k)),
            device_id_type=pl.DeviceIdType.MESH,
        )

    def vert_exchange(kind, send, recv):
        copies = [
            vert_copy(kind, k, send.at[vert_peer(k)], recv.at[my_vert]) for k in range(1, vert)
        ]
        for copy in copies:
            copy.start()
        return copies

    def vert_spread(kind, recv):
        copies = [
            vert_copy(kind, k, recv.at[my_vert], recv.at[my_vert]) for k in range(1, vert)
        ]
        for copy in copies:
            copy.start()
        return copies

    def feat_exchange(kind, send, recv):
        copies = [
            feat_copy(kind, k, send.at[feat_peer(k)], recv.at[my_feat]) for k in range(1, feat)
        ]
        for copy in copies:
            copy.start()
        return copies

    def arrived(copies):
        for copy in copies:
            copy.wait_recv()

    barrier = pltpu.get_barrier_semaphore()
    for k in range(1, vert):
        pl.semaphore_signal(
            barrier, inc=1, device_id=(vert_peer(k), my_feat), device_id_type=pl.DeviceIdType.MESH
        )
    for k in range(1, feat):
        pl.semaphore_signal(
            barrier, inc=1, device_id=(my_vert, feat_peer(k)), device_id_type=pl.DeviceIdType.MESH
        )

    half = row_count // 2
    states_copies = [
        pltpu.make_async_copy(
            states_hbm.at[:, :, pl.ds(i * half, half)],
            states_ref.at[:, :, pl.ds(i * half, half)],
            local_sem.at[i],
        )
        for i in range(2)
    ]
    weight_copy = pltpu.make_async_copy(weight_hbm, weight_ref, local_sem.at[2])
    own_cot = pltpu.make_async_copy(
        cot_hbm.at[:, pl.ds(pl.multiple_of(my_feat * width, width), width)],
        cot_recv.at[my_feat],
        local_sem.at[3],
    )
    for copy in states_copies + [weight_copy, own_cot]:
        copy.start()
    part = capacity // TILE_PARTS
    tile_copies = [
        pltpu.make_async_copy(
            tiles_hbm.at[0, pl.ds(i * part, part)], tiles.at[pl.ds(i * part, part)], tile_sem.at[i]
        )
        for i in range(TILE_PARTS)
    ]
    for copy in tile_copies:
        copy.start()

    depth = [column_of(depth_ref[j : j + 1, :]) for j in range(state_count)]
    rows = jnp.concatenate([rows_ref[0, p : p + 1, :] for p in range(vert)], axis=1)
    extended[0] = jnp.zeros((channels, block), BF16)
    running[0] = jnp.zeros((channels, block), F32)
    step = 2 * block

    def mix(i, picked):
        start = pl.multiple_of(i * step, step)
        here_states = states_ref[:, :, pl.ds(start, step)]
        total = depth[0] * here_states[0].astype(F32)
        for j in range(1, state_count):
            total += depth[j] * here_states[j].astype(F32)
        mixed = total.astype(BF16)
        extended[2 * i + 1] = mixed[:, :block]
        extended[2 * i + 2] = mixed[:, block:]
        here = lax.broadcasted_iota(jnp.int32, (step, slots), 0) + start
        onehot = jnp.where(here == rows, 1.0, 0.0).astype(BF16)
        return picked + jnp.dot(
            here_states.reshape(state_count * channels, step), onehot, preferred_element_type=F32
        )

    steps = row_count // step
    states_copies[0].wait()
    picked = lax.fori_loop(
        0, steps // 2, mix, jnp.zeros((state_count * channels, slots), F32), unroll=MIX_UNROLL
    )
    states_copies[1].wait()
    picked = lax.fori_loop(steps // 2, steps, mix, picked, unroll=MIX_UNROLL)
    picked = picked.reshape(state_count, channels, slots)
    listed = depth[0] * picked[0]
    for j in range(1, state_count):
        listed += depth[j] * picked[j]
    listed = listed.astype(BF16)
    picked_states[...] = picked

    def widened(part):
        return jnp.concatenate([part] * per_block, axis=1)

    for p in range(vert):
        halo_send[p] = widened(listed[:, p * halo : (p + 1) * halo])

    pl.semaphore_wait(barrier, vert + feat - 2)
    halo_copies = vert_exchange(HALO_OUT, halo_send, halo_recv)
    cot_copies = [
        feat_copy(
            COT,
            k,
            cot_hbm.at[:, pl.ds(pl.multiple_of(feat_peer(k) * width, width), width)],
            cot_recv.at[my_feat],
        )
        for k in range(1, feat)
    ]
    bias_recv[my_feat] = jnp.broadcast_to(column_of(bias_ref[...]), (channels, block))
    bias_copies = [
        feat_copy(BIAS, k, bias_recv.at[my_feat], bias_recv.at[my_feat]) for k in range(1, feat)
    ]
    for copy in cot_copies + bias_copies:
        copy.start()
    halo_recv[my_vert] = halo_send[my_vert]
    plan_tiles(count_ref[0], dst_ref[...], src_ref[...], plan_vec, keep_vec)
    plan_copy = pltpu.make_async_copy(plan_vec, plan, local_sem.at[4])
    plan_copy.start()
    keep_copy = pltpu.make_async_copy(keep_vec, keep, local_sem.at[5])
    keep_copy.start()
    weight_copy.wait()
    own_cot.wait()
    weight = weight_ref[...]
    weight_t[...] = weight.astype(F32).T.astype(BF16)

    arrived(halo_copies)
    for j in range(src_blocks - row_blocks):
        extended[row_blocks + j + 1] = jnp.concatenate(
            [halo_recv[j * per_block + h, :, :halo] for h in range(per_block)], axis=1
        )
    for copy in tile_copies:
        copy.wait()

    plan_copy.wait()
    keep_copy.wait()

    def closing(row, n):
        return running[jnp.clip(plan[row, n], 0, running.shape[0] - 1)]

    def tile_pass(row, source, dims, between):
        def pick(k):
            word = plan[row, k]
            tile = tiles[jnp.minimum(lax.shift_right_logical(word, 7), capacity - 1)]
            own = jnp.minimum(lax.bitwise_and(word, STRIDE - 1), source.shape[0] - 1)
            return source[own], tile

        def group(g, total):
            products = []
            for u in range(GROUP):
                k = g * GROUP + u
                left, left_tile = pick(2 * k)
                right, right_tile = pick(2 * k + 1)
                products.append(
                    lax.dot_general(
                        jnp.concatenate([left, right], axis=1),
                        jnp.concatenate([left_tile, right_tile], axis=dims),
                        (((1,), (dims,)), ((), ())),
                        preferred_element_type=F32,
                    )
                )
            for u in range(GROUP):
                k = g * GROUP + u
                total = total * keep[row, 2 * k] + products[u]
                running[k + 1] = total
            return total

        groups = (running.shape[0] - 1) // GROUP
        total = jnp.zeros((channels, block), F32)
        if between is None:
            lax.fori_loop(0, groups, group, total, unroll=REPEAT)
        else:
            middle = groups * 3 // 5
            total = lax.fori_loop(0, middle, group, total, unroll=REPEAT)
            between()
            lax.fori_loop(middle, groups, group, total, unroll=REPEAT)

    tile_pass(0, extended, 1, None)
    for n in range(row_blocks):
        part, f, columns = spot_of(n)
        agg_send[part, f, :, columns] = closing(1, n).astype(BF16)
    agg_copies = [
        feat_exchange((AGG, AGG_B)[part], agg_send.at[part], agg_recv.at[part])
        for part in range(parts)
    ]
    for part in range(parts):
        agg_recv[part, my_feat] = agg_send[part, my_feat]
    arrived(cot_copies)
    arrived(bias_copies)
    bias = bias_recv[...].reshape(features, block)[:, :1]

    grad_copies = []
    pieces = []
    for part in range(parts):
        columns = slice(part * part_width, (part + 1) * part_width)
        arrived(agg_copies[part])
        aggregated = agg_recv[part].reshape(features, part_width)
        pre_act = jnp.dot(weight_t[...], aggregated, preferred_element_type=F32) + bias
        sigmoid_pre = jax.nn.sigmoid(pre_act)
        grad_pre = (
            cot_recv[:, :, columns].reshape(features, part_width).astype(F32)
            * sigmoid_pre
            * (1.0 + pre_act * (1.0 - sigmoid_pre))
        ).astype(BF16)
        grad_send[part] = (
            jnp.dot(weight, grad_pre, preferred_element_type=F32)
            .astype(BF16)
            .reshape(feat, channels, part_width)
        )
        grad_copies.append(
            feat_exchange((GRAD, GRAD_B)[part], grad_send.at[part], grad_recv.at[part])
        )
        grad_recv[part, my_feat] = grad_send[part, my_feat]
        layer_send[:, :, columns] = (
            (pre_act * sigmoid_pre).astype(BF16).reshape(feat, channels, part_width)
        )
        pieces.append((aggregated, grad_pre))
    weight_terms = jnp.zeros((features, features), F32)
    bias_terms = jnp.zeros((features, 1), F32)
    for aggregated, grad_pre in pieces:
        weight_terms += lax.dot_general(
            aggregated, grad_pre, (((1,), (1,)), ((), ())), preferred_element_type=F32
        )
        bias_terms += jnp.sum(grad_pre.astype(F32), axis=1, keepdims=True)
    terms_send[:, :, :features] = weight_terms.astype(BF16).reshape(feat, channels, features)
    terms_send[:, :, features:] = (
        jnp.broadcast_to(bias_terms, (features, block)).astype(BF16).reshape(feat, channels, block)
    )
    terms_copies = feat_exchange(TERMS, terms_send, terms_recv)
    terms_recv[my_feat] = terms_send[my_feat]
    layer_copies = feat_exchange(LAYER, layer_send, layer_recv)
    layer_recv[my_feat] = layer_send[my_feat]

    grad_blocks[0] = jnp.zeros((channels, block), BF16)
    rows_col = jnp.broadcast_to(rows.astype(F32), (block, slots)).T[:, :1].astype(jnp.int32)

    for copies in grad_copies:
        arrived(copies)
    for n in range(row_blocks):
        part, f, columns = spot_of(n)
        grad_blocks[n + 1] = grad_recv[part, f, :, columns]
    sums_copies = []

    def send_sums():
        arrived(terms_copies)
        total = terms_recv[0].astype(F32)
        for f in range(1, feat):
            total += terms_recv[f].astype(F32)
        sums_recv[my_vert] = total
        sums_copies.extend(vert_spread(SUMS, sums_recv))

    tile_pass(2, grad_blocks, 0, send_sums)

    for s in range(row_blocks, src_blocks):
        value = closing(3, s).astype(BF16)
        for h in range(per_block):
            back_send[(s - row_blocks) * per_block + h] = widened(
                value[:, h * halo : (h + 1) * halo]
            )
    back_copies = vert_exchange(HALO_BACK, back_send, back_recv)
    back_recv[my_vert] = back_send[my_vert]
    for s in range(row_blocks):
        mixed_grad[:, s * block : (s + 1) * block] = closing(3, s)

    def own_sums(i, sums):
        start = pl.multiple_of(i * step, step)
        own = mixed_grad[:, pl.ds(start, step)]
        out = []
        for j in range(state_count):
            term = states_ref[j, :, pl.ds(start, step)].astype(F32) * own
            out.append(sums[j] + term[:, :block] + term[:, block:])
        return tuple(out)

    sums = lax.fori_loop(
        0,
        steps,
        own_sums,
        tuple(jnp.zeros((channels, block), F32) for _ in range(state_count)),
        unroll=4,
    )
    own_depth = [jnp.sum(part, axis=1, keepdims=True) for part in sums]

    arrived(back_copies)
    returned = jnp.concatenate([back_recv[q, :, :halo] for q in range(vert)], axis=1)
    returned32 = returned.astype(F32)
    depth_recv[my_vert] = jnp.zeros(depth_recv.shape[1:], F32)
    for j in range(state_count):
        listed_sum = jnp.sum(picked_states[j] * returned32, axis=1, keepdims=True)
        depth_recv[my_vert, j : j + 1, :channels] = row_of(own_depth[j] + listed_sum)
    depth_copies = vert_spread(DEPTH, depth_recv)

    def finish(i, carry):
        start = pl.multiple_of(i * step, step)
        here = lax.broadcasted_iota(jnp.int32, (slots, step), 1) + start
        onehot = jnp.where(here == rows_col, 1.0, 0.0).astype(BF16)
        mixed_grad[:, pl.ds(start, step)] += jnp.dot(
            returned, onehot, preferred_element_type=F32
        )
        return carry

    lax.fori_loop(0, steps, finish, 0, unroll=MIX_UNROLL)
    arrived(layer_copies)
    for f in range(feat):
        layer_ref[:, f * width : (f + 1) * width] = layer_recv[f]

    arrived(sums_copies)
    total = sums_recv[0]
    for q in range(1, vert):
        total += sums_recv[q]
    grad_weight_ref[...] = total[:, :features] * norm_scale
    grad_bias_ref[...] = row_of(total[:, features : features + 1] * norm_scale)
    arrived(depth_copies)
    total = depth_recv[0]
    for q in range(1, vert):
        total += depth_recv[q]
    grad_depth_ref[...] = total[:state_count, :channels] * norm_scale
    for copies in (
        halo_copies,
        cot_copies,
        bias_copies,
        *agg_copies,
        *grad_copies,
        layer_copies,
        terms_copies,
        back_copies,
        sums_copies,
        depth_copies,
    ):
        for copy in copies:
            copy.wait_send()


def output_kernel(
    layer, mixed_grad, grad_weight, grad_bias, grad_depth, depth_ref, layer_out, states_out, *outs
):
    layer_out[...] = layer[...]
    for ref, out in zip((grad_weight, grad_bias, grad_depth), outs):
        out[...] = ref[...]
    for j in range(depth_ref.shape[0]):
        scale = column_of(depth_ref[j : j + 1, :])
        states_out[j] = (scale * mixed_grad[...]).astype(BF16)


def local(
    states,
    depth_weight,
    tile_values,
    tile_dst,
    tile_src,
    tile_count,
    send_rows,
    weight,
    bias_vec,
    cotangent,
):
    state_count, channels, row_count = states.shape
    capacity, block = tile_values.shape[1], tile_values.shape[2]
    vert, feat = lax.axis_size("vert"), lax.axis_size("feat")
    halo = send_rows.shape[2]
    slots = send_rows.shape[1] * halo
    width = row_count // feat
    features = channels * feat
    row_blocks = row_count // block
    src_blocks = (row_count + slots) // block
    norm_scale = 1.0 / math.sqrt(vert * row_count)

    vmem = pl.BlockSpec(memory_space=pltpu.VMEM)
    smem = pl.BlockSpec(memory_space=pltpu.SMEM)
    most = max(vert, feat)
    terms = features + block
    parts = 2 if width % (2 * block) == 0 else 1
    hbm = pl.BlockSpec(memory_space=pltpu.HBM)
    pairs = -(-((capacity + src_blocks) // 2) // GROUP) * GROUP
    lanes = -(-2 * pairs // block) * block
    layer, mixed_grad, grad_weight, grad_bias, grad_depth = pl.pallas_call(
        functools.partial(
            whole_kernel, (vert, feat, channels, row_count, block, halo), norm_scale
        ),
        out_shape=(
            jax.ShapeDtypeStruct((channels, row_count), BF16),
            jax.ShapeDtypeStruct((channels, row_count), F32),
            jax.ShapeDtypeStruct((channels, features), F32),
            jax.ShapeDtypeStruct((1, channels), F32),
            jax.ShapeDtypeStruct((state_count, channels), F32),
        ),
        in_specs=[smem] + [vmem] * 4 + [hbm, vmem] + [hbm] * 3,
        out_specs=(vmem,) * 5,
        scratch_shapes=[
            pltpu.VMEM((capacity, block, block), BF16),
            pltpu.VMEM((src_blocks + 1, channels, block), BF16),
            pltpu.VMEM((pairs + 1, channels, block), F32),
            pltpu.VMEM((vert, channels, block), BF16),
            pltpu.VMEM((vert, channels, block), BF16),
            pltpu.VMEM((vert, channels, block), BF16),
            pltpu.VMEM((vert, channels, block), BF16),
            pltpu.VMEM((feat, channels, width), BF16),
            pltpu.VMEM((feat, channels, block), F32),
            pltpu.VMEM((parts, feat, channels, width // parts), BF16),
            pltpu.VMEM((parts, feat, channels, width // parts), BF16),
            pltpu.VMEM((parts, feat, channels, width // parts), BF16),
            pltpu.VMEM((parts, feat, channels, width // parts), BF16),
            pltpu.VMEM((feat, channels, width), BF16),
            pltpu.VMEM((feat, channels, width), BF16),
            pltpu.VMEM((feat, channels, terms), BF16),
            pltpu.VMEM((feat, channels, terms), BF16),
            pltpu.VMEM((vert, channels, terms), F32),
            pltpu.VMEM((vert, 8 * -(-state_count // 8), block), F32),
            pltpu.VMEM((row_blocks + 1, channels, block), BF16),
            pltpu.VMEM((features, features), BF16),
            pltpu.VMEM((features, features), BF16),
            pltpu.VMEM((state_count, channels, row_count), BF16),
            pltpu.VMEM((8, lanes), jnp.int32),
            pltpu.SMEM((8, lanes), jnp.int32),
            pltpu.VMEM((8, lanes), F32),
            pltpu.SMEM((8, lanes), F32),
            pltpu.VMEM((state_count, channels, slots), F32),
            pltpu.SemaphoreType.DMA((TILE_PARTS,)),
            pltpu.SemaphoreType.DMA((6,)),
            pltpu.SemaphoreType.DMA((12, most)),
            pltpu.SemaphoreType.DMA((12, most)),
        ],
        compiler_params=pltpu.CompilerParams(
            collective_id=0, has_side_effects=True, vmem_limit_bytes=VMEM_LIMIT
        ),
    )(
        tile_count,
        tile_dst,
        tile_src,
        depth_weight,
        send_rows,
        weight,
        bias_vec[None, :],
        states,
        cotangent,
        tile_values,
    )
    layer_out, grad_states, grad_weight, grad_bias, grad_depth = pl.pallas_call(
        output_kernel,
        out_shape=(
            jax.ShapeDtypeStruct((channels, row_count), BF16),
            jax.ShapeDtypeStruct((state_count, channels, row_count), BF16),
            jax.ShapeDtypeStruct((channels, features), F32),
            jax.ShapeDtypeStruct((1, channels), F32),
            jax.ShapeDtypeStruct((state_count, channels), F32),
        ),
        in_specs=[vmem] * 6,
        out_specs=(vmem,) * 5,
        compiler_params=pltpu.CompilerParams(vmem_limit_bytes=VMEM_LIMIT),
    )(layer, mixed_grad, grad_weight, grad_bias, grad_depth, depth_weight)
    return layer_out, grad_states, grad_weight, grad_bias[0], grad_depth


def solution(mesh):
    placed = (
        P(None, "feat", "vert"),
        P(None, "feat"),
        P("vert", None, None, None),
        P("vert", None),
        P("vert", None),
        P("vert"),
        P("vert", None, None),
        P(),
        P("feat"),
        P("feat", "vert"),
    )
    return jax.shard_map(
        local,
        mesh=mesh,
        in_specs=placed,
        out_specs=(
            P("feat", "vert"),
            P(None, "feat", "vert"),
            P("feat", None),
            P("feat"),
            P(None, "feat"),
        ),
        check_vma=False,
    )
```

```python
import functools
import math

import jax
import jax.numpy as jnp
from jax import lax
from jax.experimental import pallas as pl
from jax.experimental.pallas import tpu as pltpu
from jax.sharding import PartitionSpec as P

F32 = jnp.float32
BF16 = jnp.bfloat16
HALO_OUT, COT, BIAS, LAYER, TERMS, HALO_BACK, SUMS, DEPTH, AGG, AGG_B, GRAD, GRAD_B = range(12)
TILE_PARTS = 8
GROUP = 10
OUT_STEPS = 4
REPEAT = 3
VMEM_LIMIT = 63 * 1024 * 1024
STRIDE = 128
MIX_UNROLL = 8


def diagonal(size):
    down = lax.broadcasted_iota(jnp.int32, (size, size), 0)
    return down == lax.broadcasted_iota(jnp.int32, (size, size), 1)


def column_of(row):
    size = row.shape[1]
    spread = jnp.broadcast_to(row, (size, size))
    return jnp.sum(jnp.where(diagonal(size), spread, 0.0), axis=1, keepdims=True)


def row_of(column):
    size = column.shape[0]
    spread = jnp.broadcast_to(column, (size, size))
    return jnp.sum(jnp.where(diagonal(size), spread, 0.0), axis=0, keepdims=True)


def plan_tiles(tile_total, dst, src, plan_vec, keep_vec):
    capacity = dst.shape[1]
    lanes = plan_vec.shape[1]
    live = lax.broadcasted_iota(jnp.int32, (1, capacity), 1) < tile_total
    dead = float(STRIDE - 1)
    dst, src = dst.astype(F32), src.astype(F32)
    dst_key, src_key = jnp.where(live, dst, dead), jnp.where(live, src, dead)
    down = lax.broadcasted_iota(jnp.int32, (STRIDE, capacity), 0)
    stacked = jnp.where(down == 0, dst_key, jnp.where(down == 1, src_key, 0.0))
    stacked = jnp.where(down == 2, dst, jnp.where(down == 3, src, stacked))
    turned = stacked.T
    square = (capacity, capacity)
    earlier = lax.broadcasted_iota(jnp.int32, square, 1) < lax.broadcasted_iota(
        jnp.int32, square, 0
    )
    place = lax.broadcasted_iota(jnp.int32, (capacity, 1), 0).astype(F32)
    bins = lax.broadcasted_iota(jnp.int32, (capacity, STRIDE), 1).astype(F32)
    spots = lax.broadcasted_iota(jnp.int32, (capacity, lanes), 1).astype(F32)
    plan_vec[...] = jnp.zeros(plan_vec.shape, jnp.int32)
    keep_vec[...] = jnp.zeros(keep_vec.shape, F32)
    for row, key_row, key, other in (
        (0, dst_key, turned[:, 0:1], turned[:, 3:4]),
        (2, src_key, turned[:, 1:2], turned[:, 2:3]),
    ):
        same = jnp.where((key_row == key) & earlier, 1.0, 0.0)
        inside = jnp.sum(same, axis=1, keepdims=True)
        counts = jnp.sum(jnp.where(bins == key, 1.0, 0.0), axis=0, keepdims=True)
        pairs = jnp.floor((counts + 1.0) * 0.5)
        first = jnp.sum(jnp.where(bins < key, pairs, 0.0), axis=1, keepdims=True)
        spot = jnp.where(key == dead, -1.0, 2.0 * first + inside)
        word = place * STRIDE + other + 1.0
        goes_on = jnp.where(inside > 0.0, 1.0, 0.0)
        keep_vec[row : row + 1, :] = jnp.sum(
            jnp.where(spots == spot, goes_on, 0.0), axis=0, keepdims=True
        )
        words = jnp.sum(jnp.where(spots == spot, word, 0.0), axis=0, keepdims=True)
        plan_vec[row : row + 1, :] = words.astype(jnp.int32)
        after = jnp.floor(spot * 0.5) + 1.0
        last = jnp.max(jnp.where(bins == key, after, 0.0), axis=0, keepdims=True)
        plan_vec[row + 1 : row + 2, :STRIDE] = last.astype(jnp.int32)


def whole_kernel(
    sizes,
    norm_scale,
    count_ref,
    dst_ref,
    src_ref,
    depth_ref,
    rows_ref,
    weight_hbm,
    bias_ref,
    states_hbm,
    cot_hbm,
    tiles_hbm,
    layer_hbm,
    mixed_hbm,
    grad_weight_ref,
    grad_bias_ref,
    grad_depth_ref,
    tiles,
    extended,
    running,
    halo_send,
    halo_recv,
    back_send,
    back_recv,
    cot_recv,
    bias_recv,
    agg_send,
    agg_recv,
    grad_send,
    grad_recv,
    layer_send,
    layer_recv,
    terms_send,
    terms_recv,
    sums_recv,
    depth_recv,
    grad_blocks,
    weight_t,
    weight_ref,
    states_ref,
    plan_vec,
    plan,
    keep_vec,
    keep,
    picked_states,
    layer_ref,
    mixed_grad,
    tile_sem,
    local_sem,
    send_sem,
    recv_sem,
):
    vert, feat, channels, row_count, block, halo = sizes
    state_count = states_ref.shape[0]
    capacity = tiles.shape[0]
    width = row_count // feat
    features = channels * feat
    row_blocks = row_count // block
    src_blocks = extended.shape[0] - 1
    slots = vert * halo
    per_block = block // halo
    per_width = width // block
    parts, part_width = agg_send.shape[0], agg_send.shape[3]
    per_part = part_width // block

    def spot_of(n):
        j = n % per_width
        start = (j % per_part) * block
        return j // per_part, n // per_width, slice(start, start + block)

    my_vert = lax.axis_index("vert")
    my_feat = lax.axis_index("feat")

    def vert_peer(k):
        return lax.rem(my_vert + k, vert)

    def feat_peer(k):
        return lax.rem(my_feat + k, feat)

    def vert_copy(kind, k, src, dst):
        return pltpu.make_async_remote_copy(
            src_ref=src,
            dst_ref=dst,
            send_sem=send_sem.at[kind, k],
            recv_sem=recv_sem.at[kind, k],
            device_id=(vert_peer(k), my_feat),
            device_id_type=pl.DeviceIdType.MESH,
        )

    def feat_copy(kind, k, src, dst):
        return pltpu.make_async_remote_copy(
            src_ref=src,
            dst_ref=dst,
            send_sem=send_sem.at[kind, k],
            recv_sem=recv_sem.at[kind, k],
            device_id=(my_vert, feat_peer(k)),
            device_id_type=pl.DeviceIdType.MESH,
        )

    def vert_exchange(kind, send, recv):
        copies = [
            vert_copy(kind, k, send.at[vert_peer(k)], recv.at[my_vert]) for k in range(1, vert)
        ]
        for copy in copies:
            copy.start()
        return copies

    def vert_spread(kind, recv):
        copies = [
            vert_copy(kind, k, recv.at[my_vert], recv.at[my_vert]) for k in range(1, vert)
        ]
        for copy in copies:
            copy.start()
        return copies

    def feat_exchange(kind, send, recv):
        copies = [
            feat_copy(kind, k, send.at[feat_peer(k)], recv.at[my_feat]) for k in range(1, feat)
        ]
        for copy in copies:
            copy.start()
        return copies

    def arrived(copies):
        for copy in copies:
            copy.wait_recv()

    barrier = pltpu.get_barrier_semaphore()
    for k in range(1, vert):
        pl.semaphore_signal(
            barrier, inc=1, device_id=(vert_peer(k), my_feat), device_id_type=pl.DeviceIdType.MESH
        )
    for k in range(1, feat):
        pl.semaphore_signal(
            barrier, inc=1, device_id=(my_vert, feat_peer(k)), device_id_type=pl.DeviceIdType.MESH
        )

    half = row_count // 2
    states_copies = [
        pltpu.make_async_copy(
            states_hbm.at[:, :, pl.ds(i * half, half)],
            states_ref.at[:, :, pl.ds(i * half, half)],
            local_sem.at[i],
        )
        for i in range(2)
    ]
    weight_copy = pltpu.make_async_copy(weight_hbm, weight_ref, local_sem.at[2])
    own_cot = pltpu.make_async_copy(
        cot_hbm.at[:, pl.ds(pl.multiple_of(my_feat * width, width), width)],
        cot_recv.at[my_feat],
        local_sem.at[3],
    )
    for copy in states_copies + [weight_copy, own_cot]:
        copy.start()
    part = capacity // TILE_PARTS
    tile_copies = [
        pltpu.make_async_copy(
            tiles_hbm.at[0, pl.ds(i * part, part)], tiles.at[pl.ds(i * part, part)], tile_sem.at[i]
        )
        for i in range(TILE_PARTS)
    ]
    for copy in tile_copies:
        copy.start()

    depth = [column_of(depth_ref[j : j + 1, :]) for j in range(state_count)]
    rows = jnp.concatenate([rows_ref[0, p : p + 1, :] for p in range(vert)], axis=1)
    extended[0] = jnp.zeros((channels, block), BF16)
    running[0] = jnp.zeros((channels, block), F32)
    step = 2 * block

    def mix(i, picked):
        start = pl.multiple_of(i * step, step)
        here_states = states_ref[:, :, pl.ds(start, step)]
        total = depth[0] * here_states[0].astype(F32)
        for j in range(1, state_count):
            total += depth[j] * here_states[j].astype(F32)
        mixed = total.astype(BF16)
        extended[2 * i + 1] = mixed[:, :block]
        extended[2 * i + 2] = mixed[:, block:]
        here = lax.broadcasted_iota(jnp.int32, (step, slots), 0) + start
        onehot = jnp.where(here == rows, 1.0, 0.0).astype(BF16)
        return picked + jnp.dot(
            here_states.reshape(state_count * channels, step), onehot, preferred_element_type=F32
        )

    steps = row_count // step
    states_copies[0].wait()
    picked = lax.fori_loop(
        0, steps // 2, mix, jnp.zeros((state_count * channels, slots), F32), unroll=MIX_UNROLL
    )
    states_copies[1].wait()
    picked = lax.fori_loop(steps // 2, steps, mix, picked, unroll=MIX_UNROLL)
    picked = picked.reshape(state_count, channels, slots)
    listed = depth[0] * picked[0]
    for j in range(1, state_count):
        listed += depth[j] * picked[j]
    listed = listed.astype(BF16)
    picked_states[...] = picked

    def widened(part):
        return jnp.concatenate([part] * per_block, axis=1)

    for p in range(vert):
        halo_send[p] = widened(listed[:, p * halo : (p + 1) * halo])

    pl.semaphore_wait(barrier, vert + feat - 2)
    halo_copies = vert_exchange(HALO_OUT, halo_send, halo_recv)
    cot_copies = [
        feat_copy(
            COT,
            k,
            cot_hbm.at[:, pl.ds(pl.multiple_of(feat_peer(k) * width, width), width)],
            cot_recv.at[my_feat],
        )
        for k in range(1, feat)
    ]
    bias_recv[my_feat] = jnp.broadcast_to(column_of(bias_ref[...]), (channels, block))
    bias_copies = [
        feat_copy(BIAS, k, bias_recv.at[my_feat], bias_recv.at[my_feat]) for k in range(1, feat)
    ]
    for copy in cot_copies + bias_copies:
        copy.start()
    halo_recv[my_vert] = halo_send[my_vert]
    plan_tiles(count_ref[0], dst_ref[...], src_ref[...], plan_vec, keep_vec)
    plan_copy = pltpu.make_async_copy(plan_vec, plan, local_sem.at[4])
    plan_copy.start()
    keep_copy = pltpu.make_async_copy(keep_vec, keep, local_sem.at[5])
    keep_copy.start()
    weight_copy.wait()
    own_cot.wait()
    weight = weight_ref[...]
    weight_t[...] = weight.astype(F32).T.astype(BF16)

    arrived(halo_copies)
    for j in range(src_blocks - row_blocks):
        extended[row_blocks + j + 1] = jnp.concatenate(
            [halo_recv[j * per_block + h, :, :halo] for h in range(per_block)], axis=1
        )
    for copy in tile_copies:
        copy.wait()

    plan_copy.wait()
    keep_copy.wait()

    def closing(row, n):
        return running[jnp.clip(plan[row, n], 0, running.shape[0] - 1)]

    def tile_pass(row, source, dims, between):
        def pick(k):
            word = plan[row, k]
            tile = tiles[jnp.minimum(lax.shift_right_logical(word, 7), capacity - 1)]
            own = jnp.minimum(lax.bitwise_and(word, STRIDE - 1), source.shape[0] - 1)
            return source[own], tile

        def group(g, total):
            products = []
            for u in range(GROUP):
                k = g * GROUP + u
                left, left_tile = pick(2 * k)
                right, right_tile = pick(2 * k + 1)
                products.append(
                    lax.dot_general(
                        jnp.concatenate([left, right], axis=1),
                        jnp.concatenate([left_tile, right_tile], axis=dims),
                        (((1,), (dims,)), ((), ())),
                        preferred_element_type=F32,
                    )
                )
            for u in range(GROUP):
                k = g * GROUP + u
                total = total * keep[row, 2 * k] + products[u]
                running[k + 1] = total
            return total

        groups = (running.shape[0] - 1) // GROUP
        total = jnp.zeros((channels, block), F32)
        if between is None:
            lax.fori_loop(0, groups, group, total, unroll=REPEAT)
        else:
            middle = groups * 3 // 5
            total = lax.fori_loop(0, middle, group, total, unroll=REPEAT)
            between()
            lax.fori_loop(middle, groups, group, total, unroll=REPEAT)

    tile_pass(0, extended, 1, None)
    for n in range(row_blocks):
        part, f, columns = spot_of(n)
        agg_send[part, f, :, columns] = closing(1, n).astype(BF16)
    agg_copies = [
        feat_exchange((AGG, AGG_B)[part], agg_send.at[part], agg_recv.at[part])
        for part in range(parts)
    ]
    for part in range(parts):
        agg_recv[part, my_feat] = agg_send[part, my_feat]
    arrived(cot_copies)
    arrived(bias_copies)
    bias = bias_recv[...].reshape(features, block)[:, :1]

    grad_copies = []
    pieces = []
    for part in range(parts):
        columns = slice(part * part_width, (part + 1) * part_width)
        arrived(agg_copies[part])
        aggregated = agg_recv[part].reshape(features, part_width)
        pre_act = jnp.dot(weight_t[...], aggregated, preferred_element_type=F32) + bias
        sigmoid_pre = jax.nn.sigmoid(pre_act)
        grad_pre = (
            cot_recv[:, :, columns].reshape(features, part_width).astype(F32)
            * sigmoid_pre
            * (1.0 + pre_act * (1.0 - sigmoid_pre))
        ).astype(BF16)
        grad_send[part] = (
            jnp.dot(weight, grad_pre, preferred_element_type=F32)
            .astype(BF16)
            .reshape(feat, channels, part_width)
        )
        grad_copies.append(
            feat_exchange((GRAD, GRAD_B)[part], grad_send.at[part], grad_recv.at[part])
        )
        grad_recv[part, my_feat] = grad_send[part, my_feat]
        layer_send[:, :, columns] = (
            (pre_act * sigmoid_pre).astype(BF16).reshape(feat, channels, part_width)
        )
        pieces.append((aggregated, grad_pre))
    weight_terms = jnp.zeros((features, features), F32)
    bias_terms = jnp.zeros((features, 1), F32)
    for aggregated, grad_pre in pieces:
        weight_terms += lax.dot_general(
            aggregated, grad_pre, (((1,), (1,)), ((), ())), preferred_element_type=F32
        )
        bias_terms += jnp.sum(grad_pre.astype(F32), axis=1, keepdims=True)
    terms_send[:, :, :features] = weight_terms.astype(BF16).reshape(feat, channels, features)
    terms_send[:, :, features:] = (
        jnp.broadcast_to(bias_terms, (features, block)).astype(BF16).reshape(feat, channels, block)
    )
    terms_copies = feat_exchange(TERMS, terms_send, terms_recv)
    terms_recv[my_feat] = terms_send[my_feat]
    layer_copies = feat_exchange(LAYER, layer_send, layer_recv)
    layer_recv[my_feat] = layer_send[my_feat]

    grad_blocks[0] = jnp.zeros((channels, block), BF16)
    rows_col = jnp.broadcast_to(rows.astype(F32), (block, slots)).T[:, :1].astype(jnp.int32)

    for copies in grad_copies:
        arrived(copies)
    for n in range(row_blocks):
        part, f, columns = spot_of(n)
        grad_blocks[n + 1] = grad_recv[part, f, :, columns]
    sums_copies = []

    def send_sums():
        arrived(terms_copies)
        total = terms_recv[0].astype(F32)
        for f in range(1, feat):
            total += terms_recv[f].astype(F32)
        sums_recv[my_vert] = total
        sums_copies.extend(vert_spread(SUMS, sums_recv))

    tile_pass(2, grad_blocks, 0, send_sums)

    for s in range(row_blocks, src_blocks):
        value = closing(3, s).astype(BF16)
        for h in range(per_block):
            back_send[(s - row_blocks) * per_block + h] = widened(
                value[:, h * halo : (h + 1) * halo]
            )
    back_copies = vert_exchange(HALO_BACK, back_send, back_recv)
    back_recv[my_vert] = back_send[my_vert]
    for s in range(row_blocks):
        mixed_grad[:, s * block : (s + 1) * block] = closing(3, s)

    def own_sums(i, sums):
        start = pl.multiple_of(i * step, step)
        own = mixed_grad[:, pl.ds(start, step)]
        out = []
        for j in range(state_count):
            term = states_ref[j, :, pl.ds(start, step)].astype(F32) * own
            out.append(sums[j] + term[:, :block] + term[:, block:])
        return tuple(out)

    sums = lax.fori_loop(
        0,
        steps,
        own_sums,
        tuple(jnp.zeros((channels, block), F32) for _ in range(state_count)),
        unroll=4,
    )
    own_depth = [jnp.sum(part, axis=1, keepdims=True) for part in sums]

    arrived(back_copies)
    returned = jnp.concatenate([back_recv[q, :, :halo] for q in range(vert)], axis=1)
    returned32 = returned.astype(F32)
    depth_recv[my_vert] = jnp.zeros(depth_recv.shape[1:], F32)
    for j in range(state_count):
        listed_sum = jnp.sum(picked_states[j] * returned32, axis=1, keepdims=True)
        depth_recv[my_vert, j : j + 1, :channels] = row_of(own_depth[j] + listed_sum)
    depth_copies = vert_spread(DEPTH, depth_recv)

    def finish(i, carry):
        start = pl.multiple_of(i * step, step)
        here = lax.broadcasted_iota(jnp.int32, (slots, step), 1) + start
        onehot = jnp.where(here == rows_col, 1.0, 0.0).astype(BF16)
        mixed_grad[:, pl.ds(start, step)] += jnp.dot(
            returned, onehot, preferred_element_type=F32
        )
        return carry

    lax.fori_loop(0, steps, finish, 0, unroll=MIX_UNROLL)
    mixed_out = pltpu.make_async_copy(mixed_grad, mixed_hbm, local_sem.at[6])
    mixed_out.start()
    arrived(layer_copies)
    for f in range(feat):
        layer_ref[:, f * width : (f + 1) * width] = layer_recv[f]
    layer_out = pltpu.make_async_copy(layer_ref, layer_hbm, local_sem.at[7])
    layer_out.start()

    arrived(sums_copies)
    total = sums_recv[0]
    for q in range(1, vert):
        total += sums_recv[q]
    grad_weight_ref[...] = total[:, :features] * norm_scale
    grad_bias_ref[...] = row_of(total[:, features : features + 1] * norm_scale)
    arrived(depth_copies)
    total = depth_recv[0]
    for q in range(1, vert):
        total += depth_recv[q]
    grad_depth_ref[...] = total[:state_count, :channels] * norm_scale
    mixed_out.wait()
    layer_out.wait()
    for copies in (
        halo_copies,
        cot_copies,
        bias_copies,
        *agg_copies,
        *grad_copies,
        layer_copies,
        terms_copies,
        back_copies,
        sums_copies,
        depth_copies,
    ):
        for copy in copies:
            copy.wait_send()


def output_kernel(
    layer, mixed_grad, grad_weight, grad_bias, grad_depth, depth_ref, layer_out, states_out, *outs
):
    layer_out[...] = layer[...]
    for ref, out in zip((grad_weight, grad_bias, grad_depth), outs):
        out[...] = ref[...]
    for j in range(depth_ref.shape[0]):
        scale = column_of(depth_ref[j : j + 1, :])
        states_out[j] = (scale * mixed_grad[...]).astype(BF16)


def local(
    states,
    depth_weight,
    tile_values,
    tile_dst,
    tile_src,
    tile_count,
    send_rows,
    weight,
    bias_vec,
    cotangent,
):
    state_count, channels, row_count = states.shape
    capacity, block = tile_values.shape[1], tile_values.shape[2]
    vert, feat = lax.axis_size("vert"), lax.axis_size("feat")
    halo = send_rows.shape[2]
    slots = send_rows.shape[1] * halo
    width = row_count // feat
    features = channels * feat
    row_blocks = row_count // block
    src_blocks = (row_count + slots) // block
    norm_scale = 1.0 / math.sqrt(vert * row_count)

    vmem = pl.BlockSpec(memory_space=pltpu.VMEM)
    smem = pl.BlockSpec(memory_space=pltpu.SMEM)
    most = max(vert, feat)
    terms = features + block
    parts = 2 if width % (2 * block) == 0 else 1
    hbm = pl.BlockSpec(memory_space=pltpu.HBM)
    pairs = -(-((capacity + src_blocks) // 2) // GROUP) * GROUP
    lanes = -(-2 * pairs // block) * block
    layer, mixed_grad, grad_weight, grad_bias, grad_depth = pl.pallas_call(
        functools.partial(
            whole_kernel, (vert, feat, channels, row_count, block, halo), norm_scale
        ),
        out_shape=(
            jax.ShapeDtypeStruct((channels, row_count), BF16),
            jax.ShapeDtypeStruct((channels, row_count), F32),
            jax.ShapeDtypeStruct((channels, features), F32),
            jax.ShapeDtypeStruct((1, channels), F32),
            jax.ShapeDtypeStruct((state_count, channels), F32),
        ),
        in_specs=[smem] + [vmem] * 4 + [hbm, vmem] + [hbm] * 3,
        out_specs=(hbm, hbm, vmem, vmem, vmem),
        scratch_shapes=[
            pltpu.VMEM((capacity, block, block), BF16),
            pltpu.VMEM((src_blocks + 1, channels, block), BF16),
            pltpu.VMEM((pairs + 1, channels, block), F32),
            pltpu.VMEM((vert, channels, block), BF16),
            pltpu.VMEM((vert, channels, block), BF16),
            pltpu.VMEM((vert, channels, block), BF16),
            pltpu.VMEM((vert, channels, block), BF16),
            pltpu.VMEM((feat, channels, width), BF16),
            pltpu.VMEM((feat, channels, block), F32),
            pltpu.VMEM((parts, feat, channels, width // parts), BF16),
            pltpu.VMEM((parts, feat, channels, width // parts), BF16),
            pltpu.VMEM((parts, feat, channels, width // parts), BF16),
            pltpu.VMEM((parts, feat, channels, width // parts), BF16),
            pltpu.VMEM((feat, channels, width), BF16),
            pltpu.VMEM((feat, channels, width), BF16),
            pltpu.VMEM((feat, channels, terms), BF16),
            pltpu.VMEM((feat, channels, terms), BF16),
            pltpu.VMEM((vert, channels, terms), F32),
            pltpu.VMEM((vert, 8 * -(-state_count // 8), block), F32),
            pltpu.VMEM((row_blocks + 1, channels, block), BF16),
            pltpu.VMEM((features, features), BF16),
            pltpu.VMEM((features, features), BF16),
            pltpu.VMEM((state_count, channels, row_count), BF16),
            pltpu.VMEM((8, lanes), jnp.int32),
            pltpu.SMEM((8, lanes), jnp.int32),
            pltpu.VMEM((8, lanes), F32),
            pltpu.SMEM((8, lanes), F32),
            pltpu.VMEM((state_count, channels, slots), F32),
            pltpu.VMEM((channels, row_count), BF16),
            pltpu.VMEM((channels, row_count), F32),
            pltpu.SemaphoreType.DMA((TILE_PARTS,)),
            pltpu.SemaphoreType.DMA((8,)),
            pltpu.SemaphoreType.DMA((12, most)),
            pltpu.SemaphoreType.DMA((12, most)),
        ],
        compiler_params=pltpu.CompilerParams(
            collective_id=0, has_side_effects=True, vmem_limit_bytes=VMEM_LIMIT
        ),
    )(
        tile_count,
        tile_dst,
        tile_src,
        depth_weight,
        send_rows,
        weight,
        bias_vec[None, :],
        states,
        cotangent,
        tile_values,
    )

    def still(shape):
        return pl.BlockSpec(shape, lambda i: (0, 0))

    moving = pl.BlockSpec((channels, row_count // OUT_STEPS), lambda i: (0, i))
    small = [still((channels, features)), still((1, channels)), still((state_count, channels))]
    layer_out, grad_states, grad_weight, grad_bias, grad_depth = pl.pallas_call(
        output_kernel,
        out_shape=(
            jax.ShapeDtypeStruct((channels, row_count), BF16),
            jax.ShapeDtypeStruct((state_count, channels, row_count), BF16),
            jax.ShapeDtypeStruct((channels, features), F32),
            jax.ShapeDtypeStruct((1, channels), F32),
            jax.ShapeDtypeStruct((state_count, channels), F32),
        ),
        grid=(OUT_STEPS,),
        in_specs=[moving, moving, *small, still(depth_weight.shape)],
        out_specs=(
            moving,
            pl.BlockSpec((state_count, channels, row_count // OUT_STEPS), lambda i: (0, 0, i)),
            *small,
        ),
        compiler_params=pltpu.CompilerParams(vmem_limit_bytes=VMEM_LIMIT),
    )(layer, mixed_grad, grad_weight, grad_bias, grad_depth, depth_weight)
    return layer_out, grad_states, grad_weight, grad_bias[0], grad_depth


def solution(mesh):
    placed = (
        P(None, "feat", "vert"),
        P(None, "feat"),
        P("vert", None, None, None),
        P("vert", None),
        P("vert", None),
        P("vert"),
        P("vert", None, None),
        P(),
        P("feat"),
        P("feat", "vert"),
    )
    return jax.shard_map(
        local,
        mesh=mesh,
        in_specs=placed,
        out_specs=(
            P("feat", "vert"),
            P(None, "feat", "vert"),
            P("feat", None),
            P("feat"),
            P(None, "feat"),
        ),
        check_vma=False,
    )
```

```python
import functools
import math

import jax
import jax.numpy as jnp
from jax import lax
from jax.experimental import pallas as pl
from jax.experimental.pallas import tpu as pltpu
from jax.sharding import PartitionSpec as P

F32 = jnp.float32
BF16 = jnp.bfloat16
HALO_OUT, COT, BIAS, LAYER, TERMS, HALO_BACK, SUMS, DEPTH, AGG, AGG_B, GRAD, GRAD_B = range(12)
TILE_PARTS = 8
GROUP = 10
REPEAT = 3
VMEM_LIMIT = 63 * 1024 * 1024
STRIDE = 128
MIX_UNROLL = 8


def diagonal(size):
    down = lax.broadcasted_iota(jnp.int32, (size, size), 0)
    return down == lax.broadcasted_iota(jnp.int32, (size, size), 1)


def column_of(row):
    size = row.shape[1]
    spread = jnp.broadcast_to(row, (size, size))
    return jnp.sum(jnp.where(diagonal(size), spread, 0.0), axis=1, keepdims=True)


def row_of(column):
    size = column.shape[0]
    spread = jnp.broadcast_to(column, (size, size))
    return jnp.sum(jnp.where(diagonal(size), spread, 0.0), axis=0, keepdims=True)


def plan_tiles(tile_total, dst, src, plan_vec, keep_vec):
    capacity = dst.shape[1]
    lanes = plan_vec.shape[1]
    live = lax.broadcasted_iota(jnp.int32, (1, capacity), 1) < tile_total
    dead = float(STRIDE - 1)
    dst, src = dst.astype(F32), src.astype(F32)
    dst_key, src_key = jnp.where(live, dst, dead), jnp.where(live, src, dead)
    down = lax.broadcasted_iota(jnp.int32, (STRIDE, capacity), 0)
    stacked = jnp.where(down == 0, dst_key, jnp.where(down == 1, src_key, 0.0))
    stacked = jnp.where(down == 2, dst, jnp.where(down == 3, src, stacked))
    turned = stacked.T
    square = (capacity, capacity)
    earlier = lax.broadcasted_iota(jnp.int32, square, 1) < lax.broadcasted_iota(
        jnp.int32, square, 0
    )
    place = lax.broadcasted_iota(jnp.int32, (capacity, 1), 0).astype(F32)
    bins = lax.broadcasted_iota(jnp.int32, (capacity, STRIDE), 1).astype(F32)
    spots = lax.broadcasted_iota(jnp.int32, (capacity, lanes), 1).astype(F32)
    plan_vec[...] = jnp.zeros(plan_vec.shape, jnp.int32)
    keep_vec[...] = jnp.zeros(keep_vec.shape, F32)
    for row, key_row, key, other in (
        (0, dst_key, turned[:, 0:1], turned[:, 3:4]),
        (2, src_key, turned[:, 1:2], turned[:, 2:3]),
    ):
        same = jnp.where((key_row == key) & earlier, 1.0, 0.0)
        inside = jnp.sum(same, axis=1, keepdims=True)
        counts = jnp.sum(jnp.where(bins == key, 1.0, 0.0), axis=0, keepdims=True)
        pairs = jnp.floor((counts + 1.0) * 0.5)
        first = jnp.sum(jnp.where(bins < key, pairs, 0.0), axis=1, keepdims=True)
        spot = jnp.where(key == dead, -1.0, 2.0 * first + inside)
        word = place * STRIDE + other + 1.0
        goes_on = jnp.where(inside > 0.0, 1.0, 0.0)
        keep_vec[row : row + 1, :] = jnp.sum(
            jnp.where(spots == spot, goes_on, 0.0), axis=0, keepdims=True
        )
        words = jnp.sum(jnp.where(spots == spot, word, 0.0), axis=0, keepdims=True)
        plan_vec[row : row + 1, :] = words.astype(jnp.int32)
        after = jnp.floor(spot * 0.5) + 1.0
        last = jnp.max(jnp.where(bins == key, after, 0.0), axis=0, keepdims=True)
        plan_vec[row + 1 : row + 2, :STRIDE] = last.astype(jnp.int32)


def whole_kernel(
    sizes,
    norm_scale,
    count_ref,
    dst_ref,
    src_ref,
    depth_ref,
    rows_ref,
    weight_hbm,
    bias_ref,
    states_hbm,
    cot_hbm,
    tiles_hbm,
    layer_hbm,
    mixed_hbm,
    grad_weight_ref,
    grad_bias_ref,
    grad_depth_ref,
    tiles,
    extended,
    running,
    halo_send,
    halo_recv,
    back_send,
    back_recv,
    cot_recv,
    bias_recv,
    agg_send,
    agg_recv,
    grad_send,
    grad_recv,
    layer_send,
    layer_recv,
    terms_send,
    terms_recv,
    sums_recv,
    depth_recv,
    grad_blocks,
    weight_t,
    weight_ref,
    states_ref,
    plan_vec,
    plan,
    keep_vec,
    keep,
    picked_states,
    layer_ref,
    mixed_grad,
    tile_sem,
    local_sem,
    send_sem,
    recv_sem,
):
    vert, feat, channels, row_count, block, halo = sizes
    state_count = states_ref.shape[0]
    capacity = tiles.shape[0]
    width = row_count // feat
    features = channels * feat
    row_blocks = row_count // block
    src_blocks = extended.shape[0] - 1
    slots = vert * halo
    per_block = block // halo
    per_width = width // block
    parts, part_width = agg_send.shape[0], agg_send.shape[3]
    per_part = part_width // block

    def spot_of(n):
        j = n % per_width
        start = (j % per_part) * block
        return j // per_part, n // per_width, slice(start, start + block)

    my_vert = lax.axis_index("vert")
    my_feat = lax.axis_index("feat")

    def vert_peer(k):
        return lax.rem(my_vert + k, vert)

    def feat_peer(k):
        return lax.rem(my_feat + k, feat)

    def vert_copy(kind, k, src, dst):
        return pltpu.make_async_remote_copy(
            src_ref=src,
            dst_ref=dst,
            send_sem=send_sem.at[kind, k],
            recv_sem=recv_sem.at[kind, k],
            device_id=(vert_peer(k), my_feat),
            device_id_type=pl.DeviceIdType.MESH,
        )

    def feat_copy(kind, k, src, dst):
        return pltpu.make_async_remote_copy(
            src_ref=src,
            dst_ref=dst,
            send_sem=send_sem.at[kind, k],
            recv_sem=recv_sem.at[kind, k],
            device_id=(my_vert, feat_peer(k)),
            device_id_type=pl.DeviceIdType.MESH,
        )

    def vert_exchange(kind, send, recv):
        copies = [
            vert_copy(kind, k, send.at[vert_peer(k)], recv.at[my_vert]) for k in range(1, vert)
        ]
        for copy in copies:
            copy.start()
        return copies

    def vert_spread(kind, recv):
        copies = [
            vert_copy(kind, k, recv.at[my_vert], recv.at[my_vert]) for k in range(1, vert)
        ]
        for copy in copies:
            copy.start()
        return copies

    def feat_exchange(kind, send, recv):
        copies = [
            feat_copy(kind, k, send.at[feat_peer(k)], recv.at[my_feat]) for k in range(1, feat)
        ]
        for copy in copies:
            copy.start()
        return copies

    def arrived(copies):
        for copy in copies:
            copy.wait_recv()

    barrier = pltpu.get_barrier_semaphore()
    for k in range(1, vert):
        pl.semaphore_signal(
            barrier, inc=1, device_id=(vert_peer(k), my_feat), device_id_type=pl.DeviceIdType.MESH
        )
    for k in range(1, feat):
        pl.semaphore_signal(
            barrier, inc=1, device_id=(my_vert, feat_peer(k)), device_id_type=pl.DeviceIdType.MESH
        )

    half = row_count // 2
    states_copies = [
        pltpu.make_async_copy(
            states_hbm.at[:, :, pl.ds(i * half, half)],
            states_ref.at[:, :, pl.ds(i * half, half)],
            local_sem.at[i],
        )
        for i in range(2)
    ]
    weight_copy = pltpu.make_async_copy(weight_hbm, weight_ref, local_sem.at[2])
    own_cot = pltpu.make_async_copy(
        cot_hbm.at[:, pl.ds(pl.multiple_of(my_feat * width, width), width)],
        cot_recv.at[my_feat],
        local_sem.at[3],
    )
    for copy in states_copies + [weight_copy, own_cot]:
        copy.start()
    part = capacity // TILE_PARTS
    tile_copies = [
        pltpu.make_async_copy(
            tiles_hbm.at[0, pl.ds(i * part, part)], tiles.at[pl.ds(i * part, part)], tile_sem.at[i]
        )
        for i in range(TILE_PARTS)
    ]
    for copy in tile_copies:
        copy.start()

    depth = [column_of(depth_ref[j : j + 1, :]) for j in range(state_count)]
    rows = jnp.concatenate([rows_ref[0, p : p + 1, :] for p in range(vert)], axis=1)
    extended[0] = jnp.zeros((channels, block), BF16)
    running[0] = jnp.zeros((channels, block), F32)
    step = 2 * block

    def mix(i, picked):
        start = pl.multiple_of(i * step, step)
        here_states = states_ref[:, :, pl.ds(start, step)]
        total = depth[0] * here_states[0].astype(F32)
        for j in range(1, state_count):
            total += depth[j] * here_states[j].astype(F32)
        mixed = total.astype(BF16)
        extended[2 * i + 1] = mixed[:, :block]
        extended[2 * i + 2] = mixed[:, block:]
        here = lax.broadcasted_iota(jnp.int32, (step, slots), 0) + start
        onehot = jnp.where(here == rows, 1.0, 0.0).astype(BF16)
        return picked + jnp.dot(
            here_states.reshape(state_count * channels, step), onehot, preferred_element_type=F32
        )

    steps = row_count // step
    states_copies[0].wait()
    picked = lax.fori_loop(
        0, steps // 2, mix, jnp.zeros((state_count * channels, slots), F32), unroll=MIX_UNROLL
    )
    states_copies[1].wait()
    picked = lax.fori_loop(steps // 2, steps, mix, picked, unroll=MIX_UNROLL)
    picked = picked.reshape(state_count, channels, slots)
    listed = depth[0] * picked[0]
    for j in range(1, state_count):
        listed += depth[j] * picked[j]
    listed = listed.astype(BF16)
    picked_states[...] = picked

    def widened(part):
        return jnp.concatenate([part] * per_block, axis=1)

    for p in range(vert):
        halo_send[p] = widened(listed[:, p * halo : (p + 1) * halo])

    pl.semaphore_wait(barrier, vert + feat - 2)
    halo_copies = vert_exchange(HALO_OUT, halo_send, halo_recv)
    cot_copies = [
        feat_copy(
            COT,
            k,
            cot_hbm.at[:, pl.ds(pl.multiple_of(feat_peer(k) * width, width), width)],
            cot_recv.at[my_feat],
        )
        for k in range(1, feat)
    ]
    bias_recv[my_feat] = jnp.broadcast_to(column_of(bias_ref[...]), (channels, block))
    bias_copies = [
        feat_copy(BIAS, k, bias_recv.at[my_feat], bias_recv.at[my_feat]) for k in range(1, feat)
    ]
    for copy in cot_copies + bias_copies:
        copy.start()
    halo_recv[my_vert] = halo_send[my_vert]
    plan_tiles(count_ref[0], dst_ref[...], src_ref[...], plan_vec, keep_vec)
    plan_copy = pltpu.make_async_copy(plan_vec, plan, local_sem.at[4])
    plan_copy.start()
    keep_copy = pltpu.make_async_copy(keep_vec, keep, local_sem.at[5])
    keep_copy.start()
    weight_copy.wait()
    own_cot.wait()
    weight = weight_ref[...]
    weight_t[...] = weight.astype(F32).T.astype(BF16)

    arrived(halo_copies)
    for j in range(src_blocks - row_blocks):
        extended[row_blocks + j + 1] = jnp.concatenate(
            [halo_recv[j * per_block + h, :, :halo] for h in range(per_block)], axis=1
        )
    for copy in tile_copies:
        copy.wait()

    plan_copy.wait()
    keep_copy.wait()

    def closing(row, n):
        return running[jnp.clip(plan[row, n], 0, running.shape[0] - 1)]

    def tile_pass(row, source, dims, between):
        def pick(k):
            word = plan[row, k]
            tile = tiles[jnp.minimum(lax.shift_right_logical(word, 7), capacity - 1)]
            own = jnp.minimum(lax.bitwise_and(word, STRIDE - 1), source.shape[0] - 1)
            return source[own], tile

        def group(g, total):
            products = []
            for u in range(GROUP):
                k = g * GROUP + u
                left, left_tile = pick(2 * k)
                right, right_tile = pick(2 * k + 1)
                products.append(
                    lax.dot_general(
                        jnp.concatenate([left, right], axis=1),
                        jnp.concatenate([left_tile, right_tile], axis=dims),
                        (((1,), (dims,)), ((), ())),
                        preferred_element_type=F32,
                    )
                )
            for u in range(GROUP):
                k = g * GROUP + u
                total = total * keep[row, 2 * k] + products[u]
                running[k + 1] = total
            return total

        groups = (running.shape[0] - 1) // GROUP
        total = jnp.zeros((channels, block), F32)
        if between is None:
            lax.fori_loop(0, groups, group, total, unroll=REPEAT)
        else:
            middle = groups * 3 // 5
            total = lax.fori_loop(0, middle, group, total, unroll=REPEAT)
            between()
            lax.fori_loop(middle, groups, group, total, unroll=REPEAT)

    tile_pass(0, extended, 1, None)
    for n in range(row_blocks):
        part, f, columns = spot_of(n)
        agg_send[part, f, :, columns] = closing(1, n).astype(BF16)
    agg_copies = [
        feat_exchange((AGG, AGG_B)[part], agg_send.at[part], agg_recv.at[part])
        for part in range(parts)
    ]
    for part in range(parts):
        agg_recv[part, my_feat] = agg_send[part, my_feat]
    arrived(cot_copies)
    arrived(bias_copies)
    bias = bias_recv[...].reshape(features, block)[:, :1]

    grad_copies = []
    pieces = []
    for part in range(parts):
        columns = slice(part * part_width, (part + 1) * part_width)
        arrived(agg_copies[part])
        aggregated = agg_recv[part].reshape(features, part_width)
        pre_act = jnp.dot(weight_t[...], aggregated, preferred_element_type=F32) + bias
        sigmoid_pre = jax.nn.sigmoid(pre_act)
        grad_pre = (
            cot_recv[:, :, columns].reshape(features, part_width).astype(F32)
            * sigmoid_pre
            * (1.0 + pre_act * (1.0 - sigmoid_pre))
        ).astype(BF16)
        grad_send[part] = (
            jnp.dot(weight, grad_pre, preferred_element_type=F32)
            .astype(BF16)
            .reshape(feat, channels, part_width)
        )
        grad_copies.append(
            feat_exchange((GRAD, GRAD_B)[part], grad_send.at[part], grad_recv.at[part])
        )
        grad_recv[part, my_feat] = grad_send[part, my_feat]
        layer_send[:, :, columns] = (
            (pre_act * sigmoid_pre).astype(BF16).reshape(feat, channels, part_width)
        )
        pieces.append((aggregated, grad_pre))
    weight_terms = jnp.zeros((features, features), F32)
    bias_terms = jnp.zeros((features, 1), F32)
    for aggregated, grad_pre in pieces:
        weight_terms += lax.dot_general(
            aggregated, grad_pre, (((1,), (1,)), ((), ())), preferred_element_type=F32
        )
        bias_terms += jnp.sum(grad_pre.astype(F32), axis=1, keepdims=True)
    terms_send[:, :, :features] = weight_terms.astype(BF16).reshape(feat, channels, features)
    terms_send[:, :, features:] = (
        jnp.broadcast_to(bias_terms, (features, block)).astype(BF16).reshape(feat, channels, block)
    )
    terms_copies = feat_exchange(TERMS, terms_send, terms_recv)
    terms_recv[my_feat] = terms_send[my_feat]
    layer_copies = feat_exchange(LAYER, layer_send, layer_recv)
    layer_recv[my_feat] = layer_send[my_feat]

    grad_blocks[0] = jnp.zeros((channels, block), BF16)
    rows_col = jnp.broadcast_to(rows.astype(F32), (block, slots)).T[:, :1].astype(jnp.int32)

    for copies in grad_copies:
        arrived(copies)
    for n in range(row_blocks):
        part, f, columns = spot_of(n)
        grad_blocks[n + 1] = grad_recv[part, f, :, columns]
    sums_copies = []

    def send_sums():
        arrived(terms_copies)
        total = terms_recv[0].astype(F32)
        for f in range(1, feat):
            total += terms_recv[f].astype(F32)
        sums_recv[my_vert] = total
        sums_copies.extend(vert_spread(SUMS, sums_recv))

    tile_pass(2, grad_blocks, 0, send_sums)

    for s in range(row_blocks, src_blocks):
        value = closing(3, s).astype(BF16)
        for h in range(per_block):
            back_send[(s - row_blocks) * per_block + h] = widened(
                value[:, h * halo : (h + 1) * halo]
            )
    back_copies = vert_exchange(HALO_BACK, back_send, back_recv)
    back_recv[my_vert] = back_send[my_vert]
    for s in range(row_blocks):
        mixed_grad[:, s * block : (s + 1) * block] = closing(3, s)

    def own_sums(i, sums):
        start = pl.multiple_of(i * step, step)
        own = mixed_grad[:, pl.ds(start, step)]
        out = []
        for j in range(state_count):
            term = states_ref[j, :, pl.ds(start, step)].astype(F32) * own
            out.append(sums[j] + term[:, :block] + term[:, block:])
        return tuple(out)

    sums = lax.fori_loop(
        0,
        steps,
        own_sums,
        tuple(jnp.zeros((channels, block), F32) for _ in range(state_count)),
        unroll=4,
    )
    own_depth = [jnp.sum(part, axis=1, keepdims=True) for part in sums]

    arrived(back_copies)
    returned = jnp.concatenate([back_recv[q, :, :halo] for q in range(vert)], axis=1)
    returned32 = returned.astype(F32)
    depth_recv[my_vert] = jnp.zeros(depth_recv.shape[1:], F32)
    for j in range(state_count):
        listed_sum = jnp.sum(picked_states[j] * returned32, axis=1, keepdims=True)
        depth_recv[my_vert, j : j + 1, :channels] = row_of(own_depth[j] + listed_sum)
    depth_copies = vert_spread(DEPTH, depth_recv)

    def finish(i, carry):
        start = pl.multiple_of(i * step, step)
        here = lax.broadcasted_iota(jnp.int32, (slots, step), 1) + start
        onehot = jnp.where(here == rows_col, 1.0, 0.0).astype(BF16)
        mixed_grad[:, pl.ds(start, step)] += jnp.dot(
            returned, onehot, preferred_element_type=F32
        )
        return carry

    lax.fori_loop(0, steps, finish, 0, unroll=MIX_UNROLL)
    mixed_out = pltpu.make_async_copy(mixed_grad, mixed_hbm, local_sem.at[6])
    mixed_out.start()
    arrived(layer_copies)
    for f in range(feat):
        layer_ref[:, f * width : (f + 1) * width] = layer_recv[f]
    layer_out = pltpu.make_async_copy(layer_ref, layer_hbm, local_sem.at[7])
    layer_out.start()

    arrived(sums_copies)
    total = sums_recv[0]
    for q in range(1, vert):
        total += sums_recv[q]
    grad_weight_ref[...] = total[:, :features] * norm_scale
    grad_bias_ref[...] = row_of(total[:, features : features + 1] * norm_scale)
    arrived(depth_copies)
    total = depth_recv[0]
    for q in range(1, vert):
        total += depth_recv[q]
    grad_depth_ref[...] = total[:state_count, :channels] * norm_scale
    mixed_out.wait()
    layer_out.wait()
    for copies in (
        halo_copies,
        cot_copies,
        bias_copies,
        *agg_copies,
        *grad_copies,
        layer_copies,
        terms_copies,
        back_copies,
        sums_copies,
        depth_copies,
    ):
        for copy in copies:
            copy.wait_send()


def output_kernel(
    layer, mixed_grad, grad_weight, grad_bias, grad_depth, depth_ref, layer_out, states_out, *outs
):
    layer_out[...] = layer[...]
    for ref, out in zip((grad_weight, grad_bias, grad_depth), outs):
        out[...] = ref[...]
    for j in range(depth_ref.shape[0]):
        scale = column_of(depth_ref[j : j + 1, :])
        states_out[j] = (scale * mixed_grad[...]).astype(BF16)


def local(
    states,
    depth_weight,
    tile_values,
    tile_dst,
    tile_src,
    tile_count,
    send_rows,
    weight,
    bias_vec,
    cotangent,
):
    state_count, channels, row_count = states.shape
    capacity, block = tile_values.shape[1], tile_values.shape[2]
    vert, feat = lax.axis_size("vert"), lax.axis_size("feat")
    halo = send_rows.shape[2]
    slots = send_rows.shape[1] * halo
    width = row_count // feat
    features = channels * feat
    row_blocks = row_count // block
    src_blocks = (row_count + slots) // block
    norm_scale = 1.0 / math.sqrt(vert * row_count)

    vmem = pl.BlockSpec(memory_space=pltpu.VMEM)
    smem = pl.BlockSpec(memory_space=pltpu.SMEM)
    most = max(vert, feat)
    terms = features + block
    parts = 2 if width % (2 * block) == 0 else 1
    hbm = pl.BlockSpec(memory_space=pltpu.HBM)
    pairs = -(-((capacity + src_blocks) // 2) // GROUP) * GROUP
    lanes = -(-2 * pairs // block) * block
    layer, mixed_grad, grad_weight, grad_bias, grad_depth = pl.pallas_call(
        functools.partial(
            whole_kernel, (vert, feat, channels, row_count, block, halo), norm_scale
        ),
        out_shape=(
            jax.ShapeDtypeStruct((channels, row_count), BF16),
            jax.ShapeDtypeStruct((channels, row_count), F32),
            jax.ShapeDtypeStruct((channels, features), F32),
            jax.ShapeDtypeStruct((1, channels), F32),
            jax.ShapeDtypeStruct((state_count, channels), F32),
        ),
        in_specs=[smem] + [vmem] * 4 + [hbm, vmem] + [hbm] * 3,
        out_specs=(hbm, hbm, vmem, vmem, vmem),
        scratch_shapes=[
            pltpu.VMEM((capacity, block, block), BF16),
            pltpu.VMEM((src_blocks + 1, channels, block), BF16),
            pltpu.VMEM((pairs + 1, channels, block), F32),
            pltpu.VMEM((vert, channels, block), BF16),
            pltpu.VMEM((vert, channels, block), BF16),
            pltpu.VMEM((vert, channels, block), BF16),
            pltpu.VMEM((vert, channels, block), BF16),
            pltpu.VMEM((feat, channels, width), BF16),
            pltpu.VMEM((feat, channels, block), F32),
            pltpu.VMEM((parts, feat, channels, width // parts), BF16),
            pltpu.VMEM((parts, feat, channels, width // parts), BF16),
            pltpu.VMEM((parts, feat, channels, width // parts), BF16),
            pltpu.VMEM((parts, feat, channels, width // parts), BF16),
            pltpu.VMEM((feat, channels, width), BF16),
            pltpu.VMEM((feat, channels, width), BF16),
            pltpu.VMEM((feat, channels, terms), BF16),
            pltpu.VMEM((feat, channels, terms), BF16),
            pltpu.VMEM((vert, channels, terms), F32),
            pltpu.VMEM((vert, 8 * -(-state_count // 8), block), F32),
            pltpu.VMEM((row_blocks + 1, channels, block), BF16),
            pltpu.VMEM((features, features), BF16),
            pltpu.VMEM((features, features), BF16),
            pltpu.VMEM((state_count, channels, row_count), BF16),
            pltpu.VMEM((8, lanes), jnp.int32),
            pltpu.SMEM((8, lanes), jnp.int32),
            pltpu.VMEM((8, lanes), F32),
            pltpu.SMEM((8, lanes), F32),
            pltpu.VMEM((state_count, channels, slots), F32),
            pltpu.VMEM((channels, row_count), BF16),
            pltpu.VMEM((channels, row_count), F32),
            pltpu.SemaphoreType.DMA((TILE_PARTS,)),
            pltpu.SemaphoreType.DMA((8,)),
            pltpu.SemaphoreType.DMA((12, most)),
            pltpu.SemaphoreType.DMA((12, most)),
        ],
        compiler_params=pltpu.CompilerParams(
            collective_id=0, has_side_effects=True, vmem_limit_bytes=VMEM_LIMIT
        ),
    )(
        tile_count,
        tile_dst,
        tile_src,
        depth_weight,
        send_rows,
        weight,
        bias_vec[None, :],
        states,
        cotangent,
        tile_values,
    )
    layer_out, grad_states, grad_weight, grad_bias, grad_depth = pl.pallas_call(
        output_kernel,
        out_shape=(
            jax.ShapeDtypeStruct((channels, row_count), BF16),
            jax.ShapeDtypeStruct((state_count, channels, row_count), BF16),
            jax.ShapeDtypeStruct((channels, features), F32),
            jax.ShapeDtypeStruct((1, channels), F32),
            jax.ShapeDtypeStruct((state_count, channels), F32),
        ),
        in_specs=[vmem] * 6,
        out_specs=(vmem,) * 5,
        compiler_params=pltpu.CompilerParams(vmem_limit_bytes=VMEM_LIMIT),
    )(layer, mixed_grad, grad_weight, grad_bias, grad_depth, depth_weight)
    return layer_out, grad_states, grad_weight, grad_bias[0], grad_depth


def solution(mesh):
    placed = (
        P(None, "feat", "vert"),
        P(None, "feat"),
        P("vert", None, None, None),
        P("vert", None),
        P("vert", None),
        P("vert"),
        P("vert", None, None),
        P(),
        P("feat"),
        P("feat", "vert"),
    )
    return jax.shard_map(
        local,
        mesh=mesh,
        in_specs=placed,
        out_specs=(
            P("feat", "vert"),
            P(None, "feat", "vert"),
            P("feat", None),
            P("feat"),
            P(None, "feat"),
        ),
        check_vma=False,
    )
```
